128 devices in a mesh: sec: 16 (over z, y), dp: 8 (over x, core).
Axes of the slice: x: 4, y: 4, z: 4, core: 2. Of those that a mesh axis runs over, the one named last changes fastest.
Arguments:
- range_features: bfloat16 [8, 1024, 64, 256], P('dp', 'sec'), may hold values from -6 to 6
- conv_weight: bfloat16 [3, 256, 256], replicated, may hold values from -0.21875 to 0.21875
- cell_cycle: int32 [1024, 64, 1], P('sec'), may hold values from 0 to 15; in each aligned block of 4096 rows (0 to 4095, 4096 to 8191, ..., all dimensions but the last counted through in order) at most 768 rows name the same one
- cell_token: int32 [1024, 64], P('sec'), may hold values from 0 to 255
- in_weight: bfloat16 [256, 1024], replicated, may hold values from -0.375 to 0.375
- qkv_weight: bfloat16 [1024, 3072], replicated, may hold values from -0.1875 to 0.1875
- out_weight: bfloat16 [1024, 1024], replicated, may hold values from -0.1875 to 0.1875
- voxel_weight: bfloat16 [1024, 2048], replicated, may hold values from -0.1875 to 0.1875
- density_weight: bfloat16 [1024, 16], replicated, may hold values from -0.1875 to 0.1875
- ray_embed: bfloat16 [16384, 128], replicated, may hold values from -1.5 to 1.5
- block_ids: int32 [16, 128, 4], P('sec'), may hold values from 0 to 31
- density_cotangent: bfloat16 [8, 4096, 16], P('dp', 'sec'), may hold values from -6 to 6
Outputs:
- depth: float32 [8, 16384], P('dp', 'sec')
- density_grad: float32 [16, 1024], replicated
The draws below stay inside these ranges and needn't reach their ends.
Inputs may be any that keep to these rules, and one draw needn't show every extreme that they name: `cell_cycle`: among the cells of one sector (4096 cells in a row), no cycle is named more than 768 times, a bound that some block reaches.
All inputs are finite; a program needn't handle non-finite values.
Results may differ from the reference program's by a relative error of at most 0.0056.
The reference program's roundings to bfloat16 on the way count: a program that leaves them out, or rounds other values in their place, can miss the bound.
Values may be sent and summed in bfloat16 or wider, within the bound.
A program may use at most 256 MiB of HBM per device.

```python
import math
import jax
import jax.numpy as jnp
import numpy as np
from jax import lax

BEAMS = 64
D_ENC = 256
D = 1024
HEADS = 16
HEAD = 64
HEIGHTS = 16
EMB = 128
KB = 4
TOKB_DEV = 256
CELLS_DEV = 4096
AZ = 1024
CAP = 768
TOKENS = 4096
RAYS = 16384
BUNDLES = 128
VBLK = 32
CLIPS = 8
N_SEC = 16


def touch_ends(values, stream_key, smallest, largest):
    longest = values.shape.index(max(values.shape))
    spots = []
    for shift in (0, 1):
        where = [jax.random.randint(jax.random.fold_in(stream_key, axis), (), 0, length) for axis, length in enumerate(values.shape)]
        where[longest] = (where[longest] + shift) % values.shape[longest]
        spots.append(tuple(where))
    return values.at[spots[0]].set(smallest).at[spots[1]].set(largest)


def level_of(stream_key, shape, split, low, high):
    gain, own = 1.0, jax.random.fold_in(stream_key, 6)
    for dim, shards_of in split:
        heights = jnp.exp(jax.random.uniform(jax.random.fold_in(own, dim), (shards_of,), jnp.float32, low / len(split), high / len(split)))
        gain = gain * jnp.repeat(heights, shape[dim] // shards_of).reshape([-1 if axis == dim else 1 for axis in range(len(shape))])
    return gain


def deal_out(stream_key, own, number, rows, number_of, top, most, lean):
    sequence = jax.random.permutation(stream_key, number_of)
    packed, usual = portions_of(number_of, rows * top, most, lean, True), portions_of(number_of, rows * top, most, lean, False)
    places = jnp.arange(number_of)

    def named(lengths, rotation):
        used = int((lengths > 0).sum())
        fixed = max(1, used // 4)
        passed = fixed + (places - fixed + rotation * (used - fixed)) % max(1, number_of - fixed)
        return jnp.zeros((number_of,), jnp.int32).at[sequence[jnp.where(places < fixed, places, passed)]].set(jnp.asarray(lengths, jnp.int32))

    lengths = jnp.where(number % 4 == 0, named(packed, number // 4), named(usual, number - number // 4 - 1))
    mixed = jax.random.permutation(jax.random.fold_in(own, 3), number_of)
    donor, sink = mixed[0:number_of // 2 * 2:2], mixed[1:number_of // 2 * 2:2]
    slack = jnp.minimum(lengths[donor] - 1, most - lengths[sink]) // 2
    slack = jnp.where((donor == sequence[0]) | (sink == sequence[0]) | (lengths[sink] == 0), 0, jnp.maximum(slack, 0))
    passed = jax.random.randint(jax.random.fold_in(own, 4), (number_of // 2,), 0, 1 << 20) % (slack + 1)
    lengths = lengths.at[donor].add(-passed).at[sink].add(passed)
    labels = jnp.searchsorted(jnp.cumsum(lengths), jnp.arange(rows * top), side="right").astype(jnp.int32)
    listing = labels.reshape(top, rows).T
    listing = listing[jax.random.permutation(jax.random.fold_in(own, 1), rows)]
    rotation = jax.random.randint(jax.random.fold_in(own, 2), (rows, 1), 0, top)
    return jnp.take_along_axis(listing, (jnp.arange(top)[None, :] + rotation) % top, axis=1)


def portions_of(count, total, limit, skew, full):
    loads = [(1 << 20) // math.isqrt(rank ** skew) + 1 for rank in range(1, count + 1)]
    largest = limit if full else min(limit, max(-(-total // count), total * loads[0] // sum(loads)))
    least = 1 if total - largest >= count - 1 else 0
    holding, surplus = [largest] + [least] * (count - 1), total - largest - least * (count - 1)
    while surplus > 0:
        movable = [i for i in range(1, count) if holding[i] < largest] or [i for i in range(1, count) if holding[i] < limit]
        pool, left = sum([loads[i] for i in movable]), surplus
        for i in movable:
            addition = min(limit - holding[i], max(1, left * loads[i] // pool), surplus)
            holding[i] = holding[i] + addition
            surplus = surplus - addition
    return np.array(holding)


def centred(key, dims, deviation, bound, pieces=(), held_as=jnp.bfloat16):
    values = jax.random.normal(key, dims, jnp.float32) * deviation
    if len(pieces) > 0:
        values = level_of(key, dims, pieces, -0.22, 0.18) * values
    return jnp.clip(values, min=-bound, max=bound).astype(held_as)


def setup_inputs(seed: int = 0) -> dict:
    key_of = jax.random.split(jax.random.key(seed), 13)
    range_features = centred(key_of[0], (CLIPS, AZ, BEAMS, D_ENC), 1.0, 6.0, ((0, 8), (1, 16)))
    conv_weight = centred(key_of[1], (3, D_ENC, D_ENC), (3 * D_ENC) ** -0.5, 0.21875)
    cell_cycle_keys = jax.random.split(jax.random.fold_in(key_of[2], 1), AZ * BEAMS // CELLS_DEV)
    cell_cycle_turns = jax.random.permutation(jax.random.fold_in(key_of[2], 3), AZ * BEAMS // CELLS_DEV)
    cell_cycle = jax.vmap(lambda own, number: deal_out(jax.random.fold_in(key_of[2], 2), own, number, CELLS_DEV, N_SEC, 1, CAP, 2))(cell_cycle_keys, cell_cycle_turns).reshape((AZ, BEAMS, 1))
    cell_token = touch_ends(jax.random.randint(key_of[3], (AZ, BEAMS), 0, TOKB_DEV), jax.random.fold_in(key_of[3], 1), 0, TOKB_DEV - 1).astype(jnp.int32)
    in_weight = centred(key_of[4], (D_ENC, D), D_ENC ** -0.5, 0.375)
    qkv_weight = centred(key_of[5], (D, 3 * D), D ** -0.5, 0.1875)
    out_weight = centred(key_of[6], (D, D), D ** -0.5, 0.1875)
    voxel_weight = centred(key_of[7], (D, HEIGHTS * EMB), D ** -0.5, 0.1875)
    density_weight = centred(key_of[8], (D, HEIGHTS), D ** -0.5, 0.1875)
    ray_embed = centred(key_of[9], (RAYS, EMB), (EMB / 9) ** -0.5, 1.5)
    block_ids = touch_ends(jax.random.randint(key_of[10], (N_SEC, BUNDLES, KB), 0, VBLK), jax.random.fold_in(key_of[10], 1), 0, VBLK - 1).astype(jnp.int32)
    density_cotangent = centred(key_of[11], (CLIPS, TOKENS, HEIGHTS), 1.0, 6.0, ((0, 8), (1, 16)))
    return dict(range_features=range_features, conv_weight=conv_weight, cell_cycle=cell_cycle, cell_token=cell_token, in_weight=in_weight, qkv_weight=qkv_weight, out_weight=out_weight, voxel_weight=voxel_weight, density_weight=density_weight, ray_embed=ray_embed, block_ids=block_ids, density_cotangent=density_cotangent)


def encode(feats, conv_weight):
    width = feats.shape[-1]
    total = jnp.zeros(feats.shape, jnp.float32)
    for k in range(3):
        rolled = jnp.roll(feats, 1 - k, axis=0)
        total = total + jnp.dot(rolled.reshape(-1, width), conv_weight[k], preferred_element_type=jnp.float32).reshape(feats.shape)
    return (feats.astype(jnp.float32) + jax.nn.gelu(total)).astype(jnp.bfloat16)

def reference(range_features, conv_weight, cell_cycle, cell_token, in_weight, qkv_weight, out_weight, voxel_weight, density_weight, ray_embed, block_ids, density_cotangent):
    gid = (cell_cycle.reshape(-1) * TOKB_DEV + cell_token.reshape(-1)).astype(jnp.int32)
    scale = HEAD ** (-0.5)

    def one_clip(args):
        feats, cotan = args
        encoded = encode(feats, conv_weight).reshape(-1, D_ENC)
        sums = jax.ops.segment_sum(encoded.astype(jnp.float32), gid, num_segments=TOKENS)
        counts = jax.ops.segment_sum(jnp.ones(gid.shape, jnp.float32), gid, num_segments=TOKENS)
        pooled = (sums / jnp.sqrt(counts + 1.0)[:, None]).astype(jnp.bfloat16)
        lifted = jnp.dot(pooled, in_weight, preferred_element_type=jnp.float32)
        normed = (lifted * lax.rsqrt(lax.optimization_barrier(jnp.mean(lifted * lifted, axis=-1, keepdims=True)) + 1e-06)).astype(jnp.bfloat16)
        qkv = jnp.dot(normed, qkv_weight, preferred_element_type=jnp.float32).astype(jnp.bfloat16)
        query_all = qkv[:, :D].reshape(TOKENS, HEADS, HEAD).transpose(1, 0, 2)
        key_all = qkv[:, D:2 * D].reshape(TOKENS, HEADS, HEAD).transpose(1, 0, 2)
        value_all = qkv[:, 2 * D:].reshape(TOKENS, HEADS, HEAD).transpose(1, 0, 2)

        def one_head(hargs):
            qh, kh, vh = hargs
            scores = jnp.dot(qh, kh.T, preferred_element_type=jnp.float32) * scale
            expo = jnp.exp(scores)
            total = lax.optimization_barrier(jnp.sum(expo, axis=-1))
            return jnp.dot(expo.astype(jnp.bfloat16), vh, preferred_element_type=jnp.float32) / total[:, None]
        ctx = lax.map(one_head, (query_all, key_all, value_all))
        ctx = ctx.transpose(1, 0, 2).reshape(TOKENS, D).astype(jnp.bfloat16)
        mixed = (normed.astype(jnp.float32) + jnp.dot(ctx, out_weight, preferred_element_type=jnp.float32)).astype(jnp.bfloat16)
        voxel = jnp.dot(mixed, voxel_weight, preferred_element_type=jnp.float32).astype(jnp.bfloat16)
        voxel = voxel.reshape(N_SEC, VBLK, 128, EMB)
        logit = jnp.dot(mixed, density_weight, preferred_element_type=jnp.float32)
        density = jax.nn.softplus(logit).reshape(N_SEC, VBLK, 128)
        rays = ray_embed.reshape(BUNDLES, 128, EMB).astype(jnp.float32)

        def one_cycle(rargs):
            vblocks, dblocks, ids = rargs
            chosen = vblocks[ids].reshape(BUNDLES, KB * 128, EMB).astype(jnp.float32)
            dens = dblocks[ids].reshape(BUNDLES, KB * 128)
            scores = jnp.einsum('nre,nve->nrv', rays, chosen)
            return lax.optimization_barrier(jnp.sum(jax.nn.softplus(scores) * dens[:, None, :], axis=-1)).reshape(RAYS)
        tau = lax.map(one_cycle, (voxel, density, block_ids)) * (4.0 / (N_SEC * KB * 128))
        before = jnp.concatenate([jnp.zeros((1, RAYS), jnp.float32), jnp.cumsum(tau, axis=0)[:-1]], axis=0)
        dist = jnp.arange(N_SEC).astype(jnp.float32) + 0.5
        depth = lax.optimization_barrier(jnp.sum(dist[:, None] * jnp.exp(-before) * (1.0 - jnp.exp(-tau)), axis=0))
        term = cotan.astype(jnp.float32) * jax.nn.sigmoid(logit)
        grad = jnp.dot(term.T, mixed.astype(jnp.float32), precision=lax.Precision.HIGHEST)
        return (depth, grad)
    depths, grads = lax.map(one_clip, (range_features, density_cotangent))
    return (depths, lax.optimization_barrier(jnp.sum(grads, axis=0)))
```

```python
import functools
import math

import jax
import jax.numpy as jnp
from jax import lax
from jax.experimental import pallas as pl
from jax.experimental.pallas import tpu as pltpu
from jax.sharding import PartitionSpec as P

D = 1024
HEADS = 16
HEAD = 64
EMB = 128
KB = 4
TOKB = 256
HEIGHTS = 16
MESH = pl.DeviceIdType.MESH
BF16 = jnp.bfloat16
F32 = jnp.float32
VMEM_LIMIT = 60 * 1024 * 1024
LOG2E = math.log2(math.e)
LN2 = math.log(2.0)


def dot(a, b):
    return jnp.dot(a, b, preferred_element_type=F32)


def dot_nt(a, b):
    return lax.dot_general(a, b, (((1,), (1,)), ((), ())), preferred_element_type=F32)


def greet(axis, n):
    me = lax.axis_index(axis)
    barrier = pltpu.get_barrier_semaphore()

    def hello(i, _):
        pl.semaphore_signal(
            barrier, inc=1, device_id={axis: lax.rem(me + i, n)}, device_id_type=MESH
        )
        return 0

    lax.fori_loop(1, n, hello, 0)


def remote(src, dst, send_sem, recv_sem, axis, peer):
    return pltpu.make_async_remote_copy(
        src_ref=src,
        dst_ref=dst,
        send_sem=send_sem,
        recv_sem=recv_sem,
        device_id={axis: peer},
        device_id_type=MESH,
    )


def swap_halves(x):
    return pltpu.roll(x, HEAD, 1)


def low_lanes(rows):
    return lax.broadcasted_iota(jnp.int32, (rows, 128), 1) < HEAD


def gelu(x):
    inner = math.sqrt(2.0 / math.pi) * (x + 0.044715 * (x * x * x))
    return x * (0.5 * (1.0 + jnp.tanh(inner)))


def softplus2(y):
    return jnp.maximum(y, 0.0) + jnp.log2(1.0 + jnp.exp2(-jnp.abs(y)))


def encode_kernel(
    n,
    cells,
    beams,
    feats,
    conv_hbm,
    gid_ref,
    in_hbm,
    qkv_hbm,
    normed_ref,
    inmsg,
    padded,
    enc,
    outbox,
    inbox,
    cnt_out,
    cnt_in,
    outmsg,
    conv_w,
    in_w,
    qkv_w,
    load_sem,
    halo_send,
    halo_recv,
    box_send,
    box_recv,
    cnt_send,
    cnt_recv,
    msg_send,
    msg_recv,
):
    me = lax.axis_index("sec")
    loads = [
        pltpu.make_async_copy(feats, padded.at[pl.ds(beams, cells)], load_sem.at[0]),
        pltpu.make_async_copy(conv_hbm, conv_w, load_sem.at[1]),
        pltpu.make_async_copy(in_hbm, in_w, load_sem.at[2]),
        pltpu.make_async_copy(qkv_hbm, qkv_w, load_sem.at[3]),
    ]
    for load in loads:
        load.start()
    greet("sec", n)
    pl.semaphore_wait(pltpu.get_barrier_semaphore(), n - 1)
    right, left = lax.rem(me + 1, n), lax.rem(me + n - 1, n)
    halos = [
        remote(
            feats.at[pl.ds(cells - beams, beams)],
            padded.at[pl.ds(0, beams)],
            halo_send.at[0],
            halo_recv.at[0],
            "sec",
            right,
        ),
        remote(
            feats.at[pl.ds(0, beams)],
            padded.at[pl.ds(beams + cells, beams)],
            halo_send.at[1],
            halo_recv.at[1],
            "sec",
            left,
        ),
    ]
    for halo in halos:
        halo.start()

    gid = gid_ref[...]
    tok_hot = jnp.where(
        lax.broadcasted_iota(jnp.int32, (TOKB, cells), 0) == (gid & (TOKB - 1)), 1.0, 0.0
    ).astype(BF16)
    cyc_hot = jnp.where(
        lax.broadcasted_iota(jnp.int32, (n, cells), 0) == (gid // TOKB), 1.0, 0.0
    ).astype(BF16)
    hist = dot_nt(cyc_hot, tok_hot)
    for r in range(n):
        cnt_out[r] = jnp.broadcast_to(hist[r : r + 1, :], (8, TOKB))

    def send_counts(i, _):
        peer = lax.rem(me + i, n)
        remote(
            cnt_out.at[peer], cnt_in.at[me], cnt_send.at[peer], cnt_recv.at[me], "sec", peer
        ).start()
        return 0

    lax.fori_loop(1, n, send_counts, 0)
    cnt_in[me] = cnt_out[me]

    rows = 8 * beams
    chunks = cells // rows

    def encode_chunk(c):
        base = pl.multiple_of(c * rows, rows)
        total = jnp.zeros((rows, enc.shape[1]), F32)
        for k in range(3):
            total = total + dot(padded[pl.ds(base + k * beams, rows), :], conv_w[k])
        own = padded[pl.ds(base + beams, rows), :].astype(F32)
        enc[pl.ds(base, rows), :] = (own + gelu(total)).astype(BF16)

    def inner_chunk(c, _):
        encode_chunk(c)
        return 0

    loads[0].wait()
    loads[1].wait()
    lax.fori_loop(1, chunks - 1, inner_chunk, 0)
    for halo in halos:
        halo.wait()

    def edge_chunk(i, _):
        encode_chunk(i * (chunks - 1))
        return 0

    lax.fori_loop(0, 2, edge_chunk, 0)

    def pool(i, _):
        peer = lax.rem(me + i, n)
        hot = jnp.where(
            lax.broadcasted_iota(jnp.int32, (TOKB, cells), 0) == (gid_ref[...] - peer * TOKB),
            1.0,
            0.0,
        ).astype(BF16)
        part = dot(hot, enc[...]).astype(BF16)

        @pl.when(i < n)
        def _():
            outbox[peer] = part
            remote(
                outbox.at[peer], inbox.at[me], box_send.at[peer], box_recv.at[me], "sec", peer
            ).start()

        @pl.when(i == n)
        def _():
            inbox[me] = part

        return 0

    lax.fori_loop(1, n + 1, pool, 0)

    def arrive(i, _):
        peer = lax.rem(me + n - i, n)
        remote(
            cnt_out.at[peer], cnt_in.at[peer], cnt_send.at[peer], cnt_recv.at[peer], "sec", peer
        ).wait()
        remote(
            outbox.at[peer], inbox.at[peer], box_send.at[peer], box_recv.at[peer], "sec", peer
        ).wait()
        return 0

    lax.fori_loop(1, n, arrive, 0)
    loads[2].wait()
    loads[3].wait()
    sums = inbox[0].astype(F32)
    counts = cnt_in[0]
    for r in range(1, n):
        sums = sums + inbox[r].astype(F32)
        counts = counts + cnt_in[r]
    root = jnp.sqrt(jnp.transpose(counts)[:, 0:1] + 1.0)
    pooled = (sums / root).astype(BF16)
    lifted = dot(pooled, in_w[...])
    normed = (
        lifted * lax.rsqrt(jnp.mean(lifted * lifted, axis=-1, keepdims=True) + 1e-06)
    ).astype(BF16)
    normed_ref[...] = normed

    low, low_half = low_lanes(TOKB), low_lanes(TOKB // 2)
    half = TOKB // 2

    def project(i, _):
        group = lax.rem(me // 4 + i, HEADS // 4)
        column = group * (4 * HEAD)
        q4, k4, v4 = (
            dot(
                normed_ref[...],
                qkv_w[:, pl.ds(pl.multiple_of(part * D + column, 4 * HEAD), 4 * HEAD)],
            )
            for part in range(3)
        )
        for pair in range(2):
            lanes = slice(pair * 128, pair * 128 + 128)
            q, k, v = q4[:, lanes], k4[:, lanes], v4[:, lanes]
            qs, ks, vs = swap_halves(q), swap_halves(k), swap_halves(v)
            head = group * 4 + pair * 2
            outmsg[head, 0:TOKB] = jnp.where(low, q, ks).astype(BF16)
            outmsg[head, TOKB : TOKB + half] = jnp.where(low_half, v[:half], vs[half:]).astype(BF16)
            outmsg[head + 1, 0:TOKB] = jnp.where(low, qs, k).astype(BF16)
            outmsg[head + 1, TOKB : TOKB + half] = jnp.where(low_half, vs[:half], v[half:]).astype(
                BF16
            )
            for one in range(2):
                peer = head + one

                @pl.when(peer != me)
                def _():
                    remote(
                        outmsg.at[peer],
                        inmsg.at[me],
                        msg_send.at[peer],
                        msg_recv.at[me],
                        "sec",
                        peer,
                    ).start()

                @pl.when(peer == me)
                def _():
                    inmsg[me] = outmsg[me]

        return 0

    lax.fori_loop(0, HEADS // 4, project, 0)

    def collect(i, _):
        peer = lax.rem(me + n - i, n)
        remote(
            outmsg.at[peer], inmsg.at[peer], msg_send.at[peer], msg_recv.at[peer], "sec", peer
        ).wait()
        return 0

    lax.fori_loop(1, n, collect, 0)


def attention_kernel(n, msg, inctx, keys, values, outctx, ctx_send, ctx_recv):
    me = lax.axis_index("sec")
    greet("sec", n)
    half = TOKB // 2
    lane = lax.broadcasted_iota(jnp.int32, (half, 128), 1)

    def unpack(r, _):
        base = pl.multiple_of(r * TOKB, TOKB)
        qk = msg[r, 0:TOKB].astype(F32)
        keys[pl.ds(base, TOKB), :] = swap_halves(qk).astype(BF16)
        v = msg[r, TOKB : TOKB + half].astype(F32)
        ones = jnp.where(lane == HEAD, 1.0, 0.0)
        values[pl.ds(base, half), :] = jnp.where(lane < HEAD, v, ones).astype(BF16)
        values[pl.ds(base + half, half), :] = jnp.where(lane < HEAD, swap_halves(v), ones).astype(
            BF16
        )
        return 0

    lax.fori_loop(0, n, unpack, 0)
    pl.semaphore_wait(pltpu.get_barrier_semaphore(), n - 1)
    rows = n * TOKB
    width = 1024
    scale = LOG2E * HEAD ** (-0.5)
    low, low_half = low_lanes(TOKB), low_lanes(half)

    def attend(i, _):
        first = 2 * lax.rem(me // 2 + 1 + i, n // 2)
        query = jnp.concatenate(
            [
                jnp.where(low, msg[first + one, 0:TOKB].astype(F32), 0.0).astype(BF16)
                for one in range(2)
            ],
            axis=0,
        )
        acc = jnp.zeros((2 * TOKB, 128), F32)
        for c in range(rows // width):
            part = slice(c * width, (c + 1) * width)
            expo = jnp.exp2(dot_nt(query, keys[part, :]) * scale).astype(BF16)
            acc = acc + dot(expo, values[part, :])
        ctx = acc / acc[:, HEAD : HEAD + 1]
        for one in range(2):
            peer = first + one
            mine = ctx[one * TOKB : (one + 1) * TOKB]
            packed = jnp.where(low_half, mine[:half], swap_halves(mine[half:])).astype(BF16)

            @pl.when(peer != me)
            def _():
                outctx[peer] = packed
                remote(
                    outctx.at[peer], inctx.at[me], ctx_send.at[peer], ctx_recv.at[me], "sec", peer
                ).start()

            @pl.when(peer == me)
            def _():
                inctx[me] = packed

        return 0

    lax.fori_loop(0, n // 2, attend, 0)

    def collect(i, _):
        peer = lax.rem(me + n - i, n)
        remote(
            outctx.at[peer], inctx.at[peer], ctx_send.at[peer], ctx_recv.at[peer], "sec", peer
        ).wait()
        return 0

    lax.fori_loop(1, n, collect, 0)


def render_kernel(
    n,
    nd,
    ids,
    inctx,
    normed,
    cotan,
    out_hbm,
    vox_hbm,
    den_w,
    rays_hbm,
    depth_ref,
    grad_ref,
    ctx,
    mixed_ref,
    vox,
    dens,
    out_w,
    vox_w,
    rays,
    tau_out,
    tau_in,
    part_out,
    part_in,
    row_out,
    row_in,
    full_out,
    full_in,
    load_sem,
    tau_send,
    tau_recv,
    part_send,
    part_recv,
    row_send,
    row_recv,
    full_send,
    full_recv,
):
    me = lax.axis_index("sec")
    clip = lax.axis_index("dp")
    loads = [
        pltpu.make_async_copy(out_hbm, out_w, load_sem.at[0]),
        pltpu.make_async_copy(vox_hbm, vox_w, load_sem.at[1]),
        pltpu.make_async_copy(rays_hbm, rays, load_sem.at[2]),
    ]
    for load in loads:
        load.start()
    greet("sec", n)
    greet("dp", nd)
    half = TOKB // 2
    low = low_lanes(half)
    for t in range(HEADS // 2):
        even, odd = inctx[2 * t].astype(F32), inctx[2 * t + 1].astype(F32)
        lanes = slice(t * 128, (t + 1) * 128)
        ctx[0:half, lanes] = jnp.where(low, even, swap_halves(odd)).astype(BF16)
        ctx[half:TOKB, lanes] = jnp.where(low, swap_halves(even), odd).astype(BF16)
    loads[0].wait()
    mixed = (normed[...].astype(F32) + dot(ctx[...], out_w[...])).astype(BF16)
    mixed_ref[...] = mixed
    logit = dot(mixed, den_w[...])
    term = cotan[...].astype(F32) * jax.nn.sigmoid(logit)
    part = lax.dot_general(
        jnp.transpose(term)[:HEIGHTS],
        mixed.astype(F32),
        (((1,), (0,)), ((), ())),
        precision=lax.Precision.HIGHEST,
        preferred_element_type=F32,
    )
    for p in range(n):
        c, h = p // 2, p % 2
        part_out[p] = part[h * 8 : h * 8 + 8, c * 128 : (c + 1) * 128]
    pl.semaphore_wait(pltpu.get_barrier_semaphore(), n - 1 + nd - 1)

    def send_part(i, _):
        peer = lax.rem(me + i, n)
        remote(
            part_out.at[peer], part_in.at[me], part_send.at[peer], part_recv.at[me], "sec", peer
        ).start()
        return 0

    lax.fori_loop(1, n, send_part, 0)
    part_in[me] = part_out[me]

    density = LN2 * softplus2(LOG2E * logit)
    loads[1].wait()
    blocks = vox.shape[0]
    for pair in range(HEIGHTS // 2):
        two = dot(mixed_ref[...], vox_w[:, pair * 256 : (pair + 1) * 256])
        vox[:, pair * 16 : pair * 16 + 16, :] = jnp.concatenate(
            [two[:, :128].reshape(blocks, 8, 128), two[:, 128:].reshape(blocks, 8, 128)], axis=1
        ).astype(BF16)
        for one in range(2):
            h = pair * 2 + one
            dens[:, h * 8 : h * 8 + 8, :] = jnp.broadcast_to(
                density[:, h : h + 1], (TOKB, 128)
            ).reshape(blocks, 8, 128)
    loads[2].wait()
    bundles = rays.shape[0] // 128
    owned = bundles // n
    factor = LN2 * 4.0 / (n * KB * 128)

    def render(i, _):
        peer = lax.rem(me + i, n)
        for y in range(owned):
            bundle = peer * owned + y
            ray = rays[pl.ds(pl.multiple_of(bundle * 128, 128), 128), :]
            total = jnp.zeros((8, 128), F32)
            for j in range(KB):
                block = ids[bundle, j]
                score = dot_nt(vox[block], ray)
                value = softplus2(score * LOG2E) * dens[block]
                total = total + jnp.sum(value.reshape(16, 8, 128), axis=0)
            tau_out[peer, y : y + 1, :] = jnp.sum(total, axis=0, keepdims=True) * factor

        @pl.when(i < n)
        def _():
            remote(
                tau_out.at[peer], tau_in.at[me], tau_send.at[peer], tau_recv.at[me], "sec", peer
            ).start()

        @pl.when(i == n)
        def _():
            tau_in[me] = tau_out[me]

        return 0

    lax.fori_loop(1, 4, render, 0)

    def wait_part(i, _):
        peer = lax.rem(me + n - i, n)
        remote(
            part_out.at[peer], part_in.at[peer], part_send.at[peer], part_recv.at[peer], "sec", peer
        ).wait()
        return 0

    lax.fori_loop(1, n, wait_part, 0)
    row = part_in[0]
    for r in range(1, n):
        row = row + part_in[r]
    row_out[...] = row
    row_in[clip] = row

    def send_row(i, _):
        peer = lax.rem(clip + i, nd)
        remote(row_out, row_in.at[clip], row_send.at[peer], row_recv.at[clip], "dp", peer).start()
        return 0

    lax.fori_loop(1, nd, send_row, 0)
    lax.fori_loop(4, 9, render, 0)

    def wait_row(i, _):
        peer = lax.rem(clip + nd - i, nd)
        remote(row_out, row_in.at[peer], row_send.at[peer], row_recv.at[peer], "dp", peer).wait()
        return 0

    lax.fori_loop(1, nd, wait_row, 0)
    full = row_in[0]
    for r in range(1, nd):
        full = full + row_in[r]
    full_out[...] = full
    full_in[me] = full

    def send_full(i, _):
        peer = lax.rem(me + i, n)
        remote(full_out, full_in.at[me], full_send.at[peer], full_recv.at[me], "sec", peer).start()
        return 0

    lax.fori_loop(1, n, send_full, 0)
    lax.fori_loop(9, n + 1, render, 0)

    def finish(i, _):
        peer = lax.rem(me + n - i, n)
        remote(
            full_out, full_in.at[peer], full_send.at[peer], full_recv.at[peer], "sec", peer
        ).wait()
        remote(
            tau_out.at[peer], tau_in.at[peer], tau_send.at[peer], tau_recv.at[peer], "sec", peer
        ).wait()
        return 0

    lax.fori_loop(1, n, finish, 0)
    for p in range(n):
        c, h = p // 2, p % 2
        grad_ref[h * 8 : h * 8 + 8, c * 128 : (c + 1) * 128] = full_in[p]
    before = jnp.zeros(tau_in.shape[1:], F32)
    depth = jnp.zeros(tau_in.shape[1:], F32)
    for r in range(n):
        tau = tau_in[r]
        depth = depth + (r + 0.5) * jnp.exp(-before) * (1.0 - jnp.exp(-tau))
        before = before + tau
    depth_ref[...] = depth


def any_space():
    return pl.BlockSpec(memory_space=pl.ANY)


def vmem():
    return pl.BlockSpec(memory_space=pltpu.VMEM)


def dma(count):
    return pltpu.SemaphoreType.DMA((count,))


def params(number):
    return pltpu.CompilerParams(
        collective_id=number, has_side_effects=True, vmem_limit_bytes=VMEM_LIMIT
    )


def shards(
    range_features,
    conv_weight,
    cell_cycle,
    cell_token,
    in_weight,
    qkv_weight,
    out_weight,
    voxel_weight,
    density_weight,
    ray_embed,
    block_ids,
    density_cotangent,
):
    _, az_dev, beams, width = range_features.shape
    n, nd = lax.axis_size("sec"), lax.axis_size("dp")
    cells = az_dev * beams
    feats = range_features.reshape(cells, width)
    gid = (cell_cycle.reshape(az_dev, beams) * TOKB + cell_token).reshape(1, cells)
    message = (n, TOKB + TOKB // 2, 128)
    normed, msg = pl.pallas_call(
        functools.partial(encode_kernel, n, cells, beams),
        out_shape=(
            jax.ShapeDtypeStruct((TOKB, D), BF16),
            jax.ShapeDtypeStruct(message, BF16),
        ),
        in_specs=[any_space(), any_space(), vmem(), any_space(), any_space()],
        out_specs=(vmem(), vmem()),
        scratch_shapes=[
            pltpu.VMEM((cells + 2 * beams, width), BF16),
            pltpu.VMEM((cells, width), BF16),
            pltpu.VMEM((n, TOKB, width), BF16),
            pltpu.VMEM((n, TOKB, width), BF16),
            pltpu.VMEM((n, 8, TOKB), F32),
            pltpu.VMEM((n, 8, TOKB), F32),
            pltpu.VMEM(message, BF16),
            pltpu.VMEM(conv_weight.shape, BF16),
            pltpu.VMEM(in_weight.shape, BF16),
            pltpu.VMEM(qkv_weight.shape, BF16),
            dma(4),
            dma(2),
            dma(2),
            dma(n),
            dma(n),
            dma(n),
            dma(n),
            dma(n),
            dma(n),
        ],
        compiler_params=params(0),
        name="encode",
    )(feats, conv_weight, gid, in_weight, qkv_weight)
    context = (n, TOKB // 2, 128)
    ctx = pl.pallas_call(
        functools.partial(attention_kernel, n),
        out_shape=jax.ShapeDtypeStruct(context, BF16),
        in_specs=[vmem()],
        out_specs=vmem(),
        scratch_shapes=[
            pltpu.VMEM((n * TOKB, 128), BF16),
            pltpu.VMEM((n * TOKB, 128), BF16),
            pltpu.VMEM(context, BF16),
            dma(n),
            dma(n),
        ],
        compiler_params=params(1),
        name="attend",
    )(msg)
    bundles = ray_embed.shape[0] // 128
    owned = bundles // n
    depth, grad = pl.pallas_call(
        functools.partial(render_kernel, n, nd),
        out_shape=(
            jax.ShapeDtypeStruct((owned, 128), F32),
            jax.ShapeDtypeStruct((HEIGHTS, D), F32),
        ),
        in_specs=[
            pl.BlockSpec(memory_space=pltpu.SMEM),
            vmem(),
            vmem(),
            vmem(),
            any_space(),
            any_space(),
            vmem(),
            any_space(),
        ],
        out_specs=(vmem(), vmem()),
        scratch_shapes=[
            pltpu.VMEM((TOKB, D), BF16),
            pltpu.VMEM((TOKB, D), BF16),
            pltpu.VMEM((TOKB * HEIGHTS // 128, 128, EMB), BF16),
            pltpu.VMEM((TOKB * HEIGHTS // 128, 128, 128), F32),
            pltpu.VMEM(out_weight.shape, BF16),
            pltpu.VMEM(voxel_weight.shape, BF16),
            pltpu.VMEM(ray_embed.shape, BF16),
            pltpu.VMEM((n, owned, 128), F32),
            pltpu.VMEM((n, owned, 128), F32),
            pltpu.VMEM((n, 8, 128), F32),
            pltpu.VMEM((n, 8, 128), F32),
            pltpu.VMEM((8, 128), F32),
            pltpu.VMEM((nd, 8, 128), F32),
            pltpu.VMEM((8, 128), F32),
            pltpu.VMEM((n, 8, 128), F32),
            dma(3),
            dma(n),
            dma(n),
            dma(n),
            dma(n),
            dma(nd),
            dma(nd),
            dma(n),
            dma(n),
        ],
        compiler_params=params(2),
        name="render",
    )(
        block_ids[0],
        ctx,
        normed,
        density_cotangent[0],
        out_weight,
        voxel_weight,
        density_weight,
        ray_embed,
    )
    return depth.reshape(1, owned * 128), grad


def solution(mesh):
    placed = (
        P("dp", "sec", None, None),
        P(),
        P("sec", None, None),
        P("sec", None),
        P(),
        P(),
        P(),
        P(),
        P(),
        P(),
        P("sec", None, None),
        P("dp", "sec", None),
    )
    return jax.shard_map(
        shards, mesh=mesh, in_specs=placed, out_specs=(P("dp", "sec"), P()), check_vma=False
    )
```

```python
import functools
import math

import jax
import jax.numpy as jnp
from jax import lax
from jax.experimental import pallas as pl
from jax.experimental.pallas import tpu as pltpu
from jax.sharding import PartitionSpec as P

D = 1024
HEADS = 16
HEAD = 64
EMB = 128
KB = 4
TOKB = 256
HEIGHTS = 16
MESH = pl.DeviceIdType.MESH
BF16 = jnp.bfloat16
F32 = jnp.float32
VMEM_LIMIT = 60 * 1024 * 1024
LOG2E = math.log2(math.e)


def dot(a, b):
    return jnp.dot(a, b, preferred_element_type=F32)


def dot_nt(a, b):
    return lax.dot_general(a, b, (((1,), (1,)), ((), ())), preferred_element_type=F32)


def greet(axis, n):
    me = lax.axis_index(axis)
    barrier = pltpu.get_barrier_semaphore()

    def hello(i, _):
        pl.semaphore_signal(
            barrier, inc=1, device_id={axis: lax.rem(me + i, n)}, device_id_type=MESH
        )
        return 0

    lax.fori_loop(1, n, hello, 0)


def remote(src, dst, send_sem, recv_sem, axis, peer):
    return pltpu.make_async_remote_copy(
        src_ref=src,
        dst_ref=dst,
        send_sem=send_sem,
        recv_sem=recv_sem,
        device_id={axis: peer},
        device_id_type=MESH,
    )


def swap_halves(x):
    return pltpu.roll(x, HEAD, 1)


def low_lanes(rows):
    return lax.broadcasted_iota(jnp.int32, (rows, 128), 1) < HEAD


def each_peer(n, me, step):
    def body(i, _):
        step(lax.rem(me + n - i, n))
        return 0

    lax.fori_loop(1, n, body, 0)


def gelu(x):
    inner = math.sqrt(2.0 / math.pi) * (x + 0.044715 * (x * x * x))
    return x * (0.5 * (1.0 + jnp.tanh(inner)))


def softplus(x):
    return jnp.maximum(x, lax.log(1.0 + jnp.exp2(jnp.minimum(x, 80.0) * LOG2E)))


def forecast_kernel(
    n,
    nd,
    cells,
    beams,
    ids,
    cyc_ref,
    tok_ref,
    den_t,
    cot_t,
    feats,
    conv_hbm,
    in_hbm,
    qkv_hbm,
    out_hbm,
    vox_hbm,
    rays_hbm,
    tau_in,
    full_in,
    gid_ref,
    padded,
    enc,
    outbox,
    inbox,
    cnt_out,
    cnt_in,
    outmsg,
    inmsg,
    normed_ref,
    queries,
    values,
    accs,
    outctx,
    inctx,
    mixed_ref,
    vox,
    dens,
    tau_out,
    part_out,
    part_in,
    row_out,
    row_in,
    full_out,
    conv_w,
    in_w,
    qkv_w,
    out_w,
    vox_w,
    rays,
    load_sem,
    halo_send,
    halo_recv,
    box_send,
    box_recv,
    cnt_send,
    cnt_recv,
    msg_send,
    msg_recv,
    ctx_send,
    ctx_recv,
    tau_send,
    tau_recv,
    part_send,
    part_recv,
    row_send,
    row_recv,
    full_send,
    full_recv,
):
    me = lax.axis_index("sec")
    clip = lax.axis_index("dp")
    greet("sec", n)
    greet("dp", nd)
    loads = [
        pltpu.make_async_copy(feats, padded.at[pl.ds(beams, cells)], load_sem.at[0]),
        pltpu.make_async_copy(conv_hbm, conv_w, load_sem.at[1]),
        pltpu.make_async_copy(in_hbm, in_w, load_sem.at[2]),
        pltpu.make_async_copy(qkv_hbm, qkv_w, load_sem.at[3]),
        pltpu.make_async_copy(out_hbm, out_w, load_sem.at[4]),
        pltpu.make_async_copy(vox_hbm, vox_w, load_sem.at[5]),
        pltpu.make_async_copy(rays_hbm, rays, load_sem.at[6]),
    ]
    for load in loads:
        load.start()

    gid = cyc_ref[...] * TOKB + tok_ref[...]
    for p in range(cells // 128):
        gid_ref[0:1, p * 128 : (p + 1) * 128] = jnp.concatenate(
            [gid[2 * p : 2 * p + 1, :], gid[2 * p + 1 : 2 * p + 2, :]], axis=1
        )
    row = gid_ref[...]
    tok_hot = jnp.where(
        lax.broadcasted_iota(jnp.int32, (TOKB, cells), 0) == (row & (TOKB - 1)), 1.0, 0.0
    ).astype(BF16)
    cyc_hot = jnp.where(
        lax.broadcasted_iota(jnp.int32, (n, cells), 0) == (row >> 8), 1.0, 0.0
    ).astype(BF16)
    hist = dot_nt(cyc_hot, tok_hot)
    for r in range(n):
        cnt_out[r] = jnp.broadcast_to(hist[r : r + 1, :], (8, TOKB))

    pl.semaphore_wait(pltpu.get_barrier_semaphore(), n - 1 + nd - 1)
    halos = [
        remote(
            feats.at[pl.ds(cells - beams, beams)],
            padded.at[pl.ds(0, beams)],
            halo_send.at[0],
            halo_recv.at[0],
            "sec",
            lax.rem(me + 1, n),
        ),
        remote(
            feats.at[pl.ds(0, beams)],
            padded.at[pl.ds(beams + cells, beams)],
            halo_send.at[1],
            halo_recv.at[1],
            "sec",
            lax.rem(me + n - 1, n),
        ),
    ]
    for halo in halos:
        halo.start()

    rows = 16 * beams
    chunks = cells // rows

    def encode_chunk(c):
        base = pl.multiple_of(c * rows, rows)
        total = jnp.zeros((rows, enc.shape[1]), F32)
        for k in range(3):
            total = total + dot(padded[pl.ds(base + k * beams, rows), :], conv_w[k])
        own = padded[pl.ds(base + beams, rows), :].astype(F32)
        enc[pl.ds(base, rows), :] = (own + gelu(total)).astype(BF16)

    loads[0].wait()
    loads[1].wait()

    def chunk(i, _):
        @pl.when(i == chunks - 2)
        def _():
            for halo in halos:
                halo.wait()

        encode_chunk(lax.rem(i + 1, chunks))
        return 0

    lax.fori_loop(0, chunks, chunk, 0)

    def pool(i, _):
        first = 2 * lax.rem(me // 2 + 1 + i, n // 2)
        hot = jnp.where(
            lax.broadcasted_iota(jnp.int32, (2 * TOKB, cells), 0) == (gid_ref[...] - first * TOKB),
            1.0,
            0.0,
        ).astype(BF16)
        both = dot(hot, enc[...]).astype(BF16)
        for one in range(2):
            peer = first + one
            part = both[one * TOKB : (one + 1) * TOKB]

            @pl.when(peer != me)
            def _():
                outbox[peer] = part
                remote(
                    outbox.at[peer], inbox.at[me], box_send.at[peer], box_recv.at[me], "sec", peer
                ).start()
                remote(
                    cnt_out.at[peer], cnt_in.at[me], cnt_send.at[peer], cnt_recv.at[me], "sec", peer
                ).start()

            @pl.when(peer == me)
            def _():
                inbox[me] = part
                cnt_in[me] = cnt_out[me]

        return 0

    lax.fori_loop(0, n // 2, pool, 0)

    last = values.shape[1] - HEAD
    ones = jnp.where(
        lax.broadcasted_iota(jnp.int32, (last, values.shape[2]), 0) == 0, 1.0, 0.0
    ).astype(BF16)
    for c in range(values.shape[0]):
        values[c, HEAD:, :] = ones
    accs[...] = jnp.zeros_like(accs)

    def arrive(peer):
        remote(
            cnt_out.at[peer], cnt_in.at[peer], cnt_send.at[peer], cnt_recv.at[peer], "sec", peer
        ).wait()
        remote(
            outbox.at[peer], inbox.at[peer], box_send.at[peer], box_recv.at[peer], "sec", peer
        ).wait()

    each_peer(n, me, arrive)
    loads[2].wait()
    loads[3].wait()
    sums = inbox[0].astype(F32)
    counts = cnt_in[0]
    for r in range(1, n):
        sums = sums + inbox[r].astype(F32)
        counts = counts + cnt_in[r]
    root = jnp.sqrt(jnp.transpose(counts)[:, 0:1] + 1.0)
    pooled = (sums / root).astype(BF16)
    lifted = dot(pooled, in_w[...])
    normed_ref[...] = (
        lifted * lax.rsqrt(jnp.mean(lifted * lifted, axis=-1, keepdims=True) + 1e-06)
    ).astype(BF16)

    low = low_lanes(TOKB)
    half = TOKB // 2
    planes = HEADS // 4

    def project(i, _):
        group = lax.rem(me // 4 + i, planes)
        column = group * (4 * HEAD)
        q4, k4, v4 = (
            dot(
                normed_ref[...],
                qkv_w[:, pl.ds(pl.multiple_of(part * D + column, 4 * HEAD), 4 * HEAD)],
            )
            for part in range(3)
        )
        q4 = q4 * HEAD ** (-0.5)
        vt = jnp.transpose(v4).astype(BF16)
        for one in range(4):
            peer = group * 4 + one
            lanes = slice(one // 2 * 128, one // 2 * 128 + 128)
            q, k = q4[:, lanes], k4[:, lanes]
            if one % 2 == 0:
                packed = jnp.where(low, q, swap_halves(k))
            else:
                packed = jnp.where(low, swap_halves(q), k)
            outmsg[peer, 0:TOKB] = packed.astype(BF16)
            mine = vt[one * HEAD : (one + 1) * HEAD]
            outmsg[peer, TOKB : TOKB + HEAD] = mine[:, :half]
            outmsg[peer, TOKB + HEAD : TOKB + 2 * HEAD] = mine[:, half:]

            @pl.when(peer != me)
            def _():
                remote(
                    outmsg.at[peer], inmsg.at[me], msg_send.at[peer], msg_recv.at[me], "sec", peer
                ).start()

            @pl.when(peer == me)
            def _():
                inmsg[me] = outmsg[me]

        return 0

    lax.fori_loop(0, planes, project, 0)

    def meet(q, k):
        acc = accs[q]
        for c in range(2):
            first = k * 4 + 2 * c
            key = jnp.concatenate([inmsg[first, 0:TOKB], inmsg[first + 1, 0:TOKB]], axis=0)
            expo = jnp.exp2(dot_nt(key, queries[q]) * LOG2E).astype(BF16)
            acc = acc + dot(values[k * 2 + c], expo)
        accs[q] = acc

    def stage(i, _):
        plane = lax.rem(me // 4 + planes - i, planes)
        for one in range(4):
            peer = plane * 4 + one

            @pl.when(peer != me)
            def _():
                remote(
                    outmsg.at[peer],
                    inmsg.at[peer],
                    msg_send.at[peer],
                    msg_recv.at[peer],
                    "sec",
                    peer,
                ).wait_recv()

            qk = inmsg[peer, 0:TOKB].astype(F32)
            queries[plane, one * TOKB : (one + 1) * TOKB] = jnp.where(
                low, 0.0, swap_halves(qk)
            ).astype(BF16)
            chunk = plane * 2 + one // 2
            base = one % 2 * TOKB
            values[chunk, 0:HEAD, base : base + half] = inmsg[peer, TOKB : TOKB + HEAD]
            values[chunk, 0:HEAD, base + half : base + TOKB] = inmsg[
                peer, TOKB + HEAD : TOKB + 2 * HEAD
            ]

        def pair(t, _):
            fresh = t >= i
            back_q = jnp.where(fresh, i, t)
            back_k = jnp.where(fresh, t - i, i)
            q = lax.rem(me // 4 + planes - back_q, planes)
            meet(q, lax.rem(me // 4 + planes - back_k, planes))

            @pl.when((i == planes - 1) & ((t < i) | (t == 2 * i)))
            def _():
                acc = accs[q]
                ctx = (acc[:HEAD] / acc[HEAD : HEAD + 1]).astype(BF16)
                for one in range(4):
                    peer = q * 4 + one
                    mine = ctx[:, one * TOKB : (one + 1) * TOKB]

                    @pl.when(peer != me)
                    def _():
                        outctx[peer] = mine
                        remote(
                            outctx.at[peer],
                            inctx.at[me],
                            ctx_send.at[peer],
                            ctx_recv.at[me],
                            "sec",
                            peer,
                        ).start()

                    @pl.when(peer == me)
                    def _():
                        inctx[me] = mine

            return 0

        lax.fori_loop(0, 2 * i + 1, pair, 0)
        return 0

    lax.fori_loop(0, planes, stage, 0)

    def context(peer):
        remote(
            outmsg.at[peer], inmsg.at[peer], msg_send.at[peer], msg_recv.at[peer], "sec", peer
        ).wait_send()
        remote(
            outctx.at[peer], inctx.at[peer], ctx_send.at[peer], ctx_recv.at[peer], "sec", peer
        ).wait()

    each_peer(n, me, context)
    for load in loads[4:]:
        load.wait()

    ctx = jnp.transpose(inctx[...].reshape(D, TOKB))
    mixed = (normed_ref[...].astype(F32) + dot(ctx, out_w[...])).astype(BF16)
    mixed_ref[...] = mixed
    term = cot_t[...].astype(F32) * jax.nn.sigmoid(dot_nt(den_t[...], mixed))
    part = lax.dot_general(
        term,
        mixed.astype(F32),
        (((1,), (0,)), ((), ())),
        precision=lax.Precision.HIGHEST,
        preferred_element_type=F32,
    )
    for p in range(n):
        c, h = p // 2, p % 2
        part_out[p] = part[h * 8 : h * 8 + 8, c * 128 : (c + 1) * 128]

    def send_part(peer):
        remote(
            part_out.at[peer], part_in.at[me], part_send.at[peer], part_recv.at[me], "sec", peer
        ).start()

    each_peer(n, me, send_part)
    part_in[me] = part_out[me]

    density = softplus(dot_nt(mixed, den_t[...]))
    blocks = vox.shape[0]
    for pair in range(HEIGHTS // 2):
        two = dot(mixed_ref[...], vox_w[:, pair * 256 : (pair + 1) * 256])
        vox[:, pair * 16 : pair * 16 + 16, :] = jnp.concatenate(
            [two[:, :128].reshape(blocks, 8, 128), two[:, 128:].reshape(blocks, 8, 128)], axis=1
        ).astype(BF16)
        for one in range(2):
            h = pair * 2 + one
            dens[:, h * 8 : h * 8 + 8, :] = jnp.broadcast_to(
                density[:, h : h + 1], (TOKB, 128)
            ).reshape(blocks, 8, 128)
    bundles = rays.shape[0] // 128
    owned = bundles // n
    factor = 4.0 / (n * KB * 128)

    def render(i, _):
        peer = lax.rem(me + i, n)
        for y in range(owned):
            bundle = peer * owned + y
            ray = rays[pl.ds(pl.multiple_of(bundle * 128, 128), 128), :]
            picks = [ids[j, bundle] for j in range(KB)]
            score = dot_nt(jnp.concatenate([vox[b] for b in picks], axis=0), ray)
            total = jnp.zeros((8, 128), F32)
            for j in range(KB):
                value = softplus(score[j * 128 : (j + 1) * 128]) * dens[picks[j]]
                total = total + jnp.sum(value.reshape(16, 8, 128), axis=0)
            tau_out[peer, y : y + 1, :] = jnp.sum(total, axis=0, keepdims=True) * factor

        @pl.when(i < n)
        def _():
            remote(
                tau_out.at[peer], tau_in.at[me], tau_send.at[peer], tau_recv.at[me], "sec", peer
            ).start()

        @pl.when(i == n)
        def _():
            tau_in[me] = tau_out[me]

        @pl.when(i == 3)
        def _():
            def wait_part(peer):
                remote(
                    part_out.at[peer],
                    part_in.at[peer],
                    part_send.at[peer],
                    part_recv.at[peer],
                    "sec",
                    peer,
                ).wait()

            each_peer(n, me, wait_part)
            row = part_in[0]
            for r in range(1, n):
                row = row + part_in[r]
            row_out[...] = row
            row_in[clip] = row

            def send_row(peer):
                remote(
                    row_out, row_in.at[clip], row_send.at[peer], row_recv.at[clip], "dp", peer
                ).start()

            each_peer(nd, clip, send_row)

        @pl.when(i == 8)
        def _():
            def wait_row(peer):
                remote(
                    row_out, row_in.at[peer], row_send.at[peer], row_recv.at[peer], "dp", peer
                ).wait()

            each_peer(nd, clip, wait_row)
            full = row_in[0]
            for r in range(1, nd):
                full = full + row_in[r]
            full_out[...] = full
            full_in[me] = full

            def send_full(peer):
                remote(
                    full_out, full_in.at[me], full_send.at[peer], full_recv.at[me], "sec", peer
                ).start()

            each_peer(n, me, send_full)

        return 0

    lax.fori_loop(1, n + 1, render, 0)

    def finish(peer):
        remote(
            full_out, full_in.at[peer], full_send.at[peer], full_recv.at[peer], "sec", peer
        ).wait()
        remote(
            tau_out.at[peer], tau_in.at[peer], tau_send.at[peer], tau_recv.at[peer], "sec", peer
        ).wait()

    each_peer(n, me, finish)


def finish_kernel(n, tau_ref, full_ref, depth_ref, grad_ref):
    for p in range(n):
        c, h = p // 2, p % 2
        grad_ref[h * 8 : h * 8 + 8, c * 128 : (c + 1) * 128] = full_ref[p]
    before = jnp.zeros(tau_ref.shape[1:], F32)
    depth = jnp.zeros(tau_ref.shape[1:], F32)
    for r in range(n):
        tau = tau_ref[r]
        depth = depth + (r + 0.5) * jnp.exp(-before) * (1.0 - jnp.exp(-tau))
        before = before + tau
    depth_ref[...] = depth


def any_space():
    return pl.BlockSpec(memory_space=pl.ANY)


def vmem():
    return pl.BlockSpec(memory_space=pltpu.VMEM)


def dma(count):
    return pltpu.SemaphoreType.DMA((count,))


def shards(
    range_features,
    conv_weight,
    cell_cycle,
    cell_token,
    in_weight,
    qkv_weight,
    out_weight,
    voxel_weight,
    density_weight,
    ray_embed,
    block_ids,
    density_cotangent,
):
    _, az_dev, beams, width = range_features.shape
    n, nd = lax.axis_size("sec"), lax.axis_size("dp")
    cells = az_dev * beams
    bundles = ray_embed.shape[0] // 128
    owned = bundles // n
    blocks = TOKB * HEIGHTS // 128
    message = (n, TOKB + TOKB // 2, 128)
    tau, full = pl.pallas_call(
        functools.partial(forecast_kernel, n, nd, cells, beams),
        out_shape=(
            jax.ShapeDtypeStruct((n, owned, 128), F32),
            jax.ShapeDtypeStruct((n, 8, 128), F32),
        ),
        in_specs=[pl.BlockSpec(memory_space=pltpu.SMEM)] + [vmem()] * 4 + [any_space()] * 7,
        out_specs=(vmem(), vmem()),
        scratch_shapes=[
            pltpu.VMEM((1, cells), jnp.int32),
            pltpu.VMEM((cells + 2 * beams, width), BF16),
            pltpu.VMEM((cells, width), BF16),
            pltpu.VMEM((n, TOKB, width), BF16),
            pltpu.VMEM((n, TOKB, width), BF16),
            pltpu.VMEM((n, 8, TOKB), F32),
            pltpu.VMEM((n, 8, TOKB), F32),
            pltpu.VMEM(message, BF16),
            pltpu.VMEM(message, BF16),
            pltpu.VMEM((TOKB, D), BF16),
            pltpu.VMEM((n // 4, 4 * TOKB, 128), BF16),
            pltpu.VMEM((n // 2, HEAD + 16, 2 * TOKB), BF16),
            pltpu.VMEM((n // 4, HEAD + 16, 4 * TOKB), F32),
            pltpu.VMEM((n, HEAD, TOKB), BF16),
            pltpu.VMEM((n, HEAD, TOKB), BF16),
            pltpu.VMEM((TOKB, D), BF16),
            pltpu.VMEM((blocks, 128, EMB), BF16),
            pltpu.VMEM((blocks, 128, 128), F32),
            pltpu.VMEM((n, owned, 128), F32),
            pltpu.VMEM((n, 8, 128), F32),
            pltpu.VMEM((n, 8, 128), F32),
            pltpu.VMEM((8, 128), F32),
            pltpu.VMEM((nd, 8, 128), F32),
            pltpu.VMEM((8, 128), F32),
            pltpu.VMEM(conv_weight.shape, BF16),
            pltpu.VMEM(in_weight.shape, BF16),
            pltpu.VMEM(qkv_weight.shape, BF16),
            pltpu.VMEM(out_weight.shape, BF16),
            pltpu.VMEM(voxel_weight.shape, BF16),
            pltpu.VMEM(ray_embed.shape, BF16),
            dma(7),
            dma(2),
            dma(2),
            dma(n),
            dma(n),
            dma(n),
            dma(n),
            dma(n),
            dma(n),
            dma(n),
            dma(n),
            dma(n),
            dma(n),
            dma(n),
            dma(n),
            dma(nd),
            dma(nd),
            dma(n),
            dma(n),
        ],
        compiler_params=pltpu.CompilerParams(
            collective_id=0, has_side_effects=True, vmem_limit_bytes=VMEM_LIMIT
        ),
        name="forecast",
    )(
        block_ids[0].T,
        cell_cycle.reshape(az_dev, beams),
        cell_token,
        density_weight.T,
        density_cotangent[0].T,
        range_features.reshape(cells, width),
        conv_weight,
        in_weight,
        qkv_weight,
        out_weight,
        voxel_weight,
        ray_embed,
    )
    depth, grad = pl.pallas_call(
        functools.partial(finish_kernel, n),
        out_shape=(
            jax.ShapeDtypeStruct((owned, 128), F32),
            jax.ShapeDtypeStruct((HEIGHTS, D), F32),
        ),
        in_specs=[vmem(), vmem()],
        out_specs=(vmem(), vmem()),
        name="finish",
    )(tau, full)
    return depth.reshape(1, owned * 128), grad


def solution(mesh):
    placed = (
        P("dp", "sec", None, None),
        P(),
        P("sec", None, None),
        P("sec", None),
        P(),
        P(),
        P(),
        P(),
        P(),
        P(),
        P("sec", None, None),
        P("dp", "sec", None),
    )
    return jax.shard_map(
        shards, mesh=mesh, in_specs=placed, out_specs=(P("dp", "sec"), P()), check_vma=False
    )
```

```python
import functools
import math

import jax
import jax.numpy as jnp
from jax import lax
from jax.experimental import pallas as pl
from jax.experimental.pallas import tpu as pltpu
from jax.sharding import PartitionSpec as P

D = 1024
HEADS = 16
HEAD = 64
EMB = 128
KB = 4
TOKB = 256
HEIGHTS = 16
MESH = pl.DeviceIdType.MESH
BF16 = jnp.bfloat16
F32 = jnp.float32
VMEM_LIMIT = 60 * 1024 * 1024
LOG2E = math.log2(math.e)


def dot(a, b):
    return jnp.dot(a, b, preferred_element_type=F32)


def dot_nt(a, b):
    return lax.dot_general(a, b, (((1,), (1,)), ((), ())), preferred_element_type=F32)


def greet(axis, n):
    me = lax.axis_index(axis)
    barrier = pltpu.get_barrier_semaphore()

    def hello(i, _):
        pl.semaphore_signal(
            barrier, inc=1, device_id={axis: lax.rem(me + i, n)}, device_id_type=MESH
        )
        return 0

    lax.fori_loop(1, n, hello, 0)


def remote(src, dst, send_sem, recv_sem, axis, peer):
    return pltpu.make_async_remote_copy(
        src_ref=src,
        dst_ref=dst,
        send_sem=send_sem,
        recv_sem=recv_sem,
        device_id={axis: peer},
        device_id_type=MESH,
    )


def swap_halves(x):
    return pltpu.roll(x, HEAD, 1)


def low_lanes(rows):
    return lax.broadcasted_iota(jnp.int32, (rows, 128), 1) < HEAD


def pick(i, choices):
    chosen = jnp.int32(choices[0])
    for k, choice in enumerate(choices[1:]):
        chosen = jnp.where(i == k + 1, choice, chosen)
    return chosen


def moved(me, dz, dy):
    return lax.rem(me // 4 + dz + 4, 4) * 4 + lax.rem(me + dy + 4, 4)


ORDER = (
    ((1, 2), (-1, 2)),
    ((2, 1), (2, -1)),
    ((1, 1), (-1, -1)),
    ((1, -1), (-1, 1)),
    ((2, 0), (0, 2)),
    ((2, 2), (1, 0)),
    ((-1, 0), (0, 1)),
    ((0, -1), (0, 0)),
)
PLANES = ((1, -1), (2, 0))
GROUPS = (
    ((1, 1), (-1, -1), (1, -1), (-1, 1)),
    ((1, 2), (-1, 2), (2, 1), (2, -1)),
    ((2, 2), (2, 0), (0, 2), (0, 0)),
    ((1, 0), (-1, 0), (0, 1), (0, -1)),
)
WINDOW = 4


def each_peer(n, me, step):
    def body(i, _):
        step(lax.rem(me + n - i, n))
        return 0

    lax.fori_loop(1, n, body, 0)


def gelu(x):
    inner = math.sqrt(2.0 / math.pi) * (x + 0.044715 * (x * x * x))
    return x * (0.5 * (1.0 + jnp.tanh(inner)))


def softplus(x):
    return jnp.maximum(x, lax.log(1.0 + jnp.exp2(jnp.minimum(x, 80.0) * LOG2E)))


def forecast_kernel(
    n,
    nd,
    cells,
    beams,
    ids,
    cyc_ref,
    tok_ref,
    den_t,
    cot_t,
    feats,
    conv_hbm,
    in_hbm,
    qkv_hbm,
    out_hbm,
    vox_hbm,
    rays_hbm,
    tau_in,
    full_in,
    gid_ref,
    padded,
    enc,
    out_y,
    in_y,
    out_z,
    in_z,
    mid_out,
    mid_in,
    cnt_out,
    cnt_in,
    outmsg,
    inmsg,
    normed_ref,
    queries,
    keys,
    values,
    accs,
    outctx,
    inctx,
    mixed_ref,
    vox,
    dens,
    tau_out,
    part_out,
    part_in,
    row_out,
    row_in,
    full_out,
    conv_w,
    in_w,
    qkv_w,
    out_w,
    vox_w,
    rays,
    load_sem,
    halo_send,
    halo_recv,
    box_send,
    box_recv,
    mid_send,
    mid_recv,
    cnt_send,
    cnt_recv,
    msg_send,
    msg_recv,
    ctx_send,
    ctx_recv,
    tau_send,
    tau_recv,
    part_send,
    part_recv,
    row_send,
    row_recv,
    full_send,
    full_recv,
):
    me = lax.axis_index("sec")
    clip = lax.axis_index("dp")
    greet("sec", n)
    greet("dp", nd)
    loads = [
        pltpu.make_async_copy(feats, padded.at[pl.ds(beams, cells)], load_sem.at[0]),
        pltpu.make_async_copy(conv_hbm, conv_w, load_sem.at[1]),
        pltpu.make_async_copy(in_hbm, in_w, load_sem.at[2]),
        pltpu.make_async_copy(qkv_hbm, qkv_w, load_sem.at[3]),
        pltpu.make_async_copy(out_hbm, out_w, load_sem.at[4]),
        pltpu.make_async_copy(vox_hbm, vox_w, load_sem.at[5]),
        pltpu.make_async_copy(rays_hbm, rays, load_sem.at[6]),
    ]
    for load in loads[:2]:
        load.start()
    gid = cyc_ref[...] * TOKB + tok_ref[...]
    for p in range(cells // 128):
        gid_ref[0:1, p * 128 : (p + 1) * 128] = jnp.concatenate(
            [gid[2 * p : 2 * p + 1, :], gid[2 * p + 1 : 2 * p + 2, :]], axis=1
        )
    pl.semaphore_wait(pltpu.get_barrier_semaphore(), n - 1 + nd - 1)
    halos = [
        remote(
            feats.at[pl.ds(cells - beams, beams)],
            padded.at[pl.ds(0, beams)],
            halo_send.at[0],
            halo_recv.at[0],
            "sec",
            lax.rem(me + 1, n),
        ),
        remote(
            feats.at[pl.ds(0, beams)],
            padded.at[pl.ds(beams + cells, beams)],
            halo_send.at[1],
            halo_recv.at[1],
            "sec",
            lax.rem(me + n - 1, n),
        ),
    ]
    for halo in halos:
        halo.start()

    rows = 16 * beams
    chunks = cells // rows

    def encode_chunk(c):
        base = pl.multiple_of(c * rows, rows)
        total = jnp.zeros((rows, enc.shape[1]), F32)
        for k in range(3):
            total = total + dot(padded[pl.ds(base + k * beams, rows), :], conv_w[k])
        own = padded[pl.ds(base + beams, rows), :].astype(F32)
        enc[pl.ds(base, rows), :] = (own + gelu(total)).astype(BF16)

    loads[0].wait()
    loads[1].wait()
    for load in loads[2:]:
        load.start()

    def chunk(i, _):
        @pl.when(i == chunks - 2)
        def _():
            for halo in halos:
                halo.wait()

        encode_chunk(lax.rem(i + 1, chunks))
        return 0

    lax.fori_loop(0, chunks, chunk, 0)

    mz, my = me // 4, lax.rem(me, 4)
    wide = enc.shape[1] // 2

    def along_y(ty, tz, slot):
        return remote(
            out_y.at[ty, tz],
            in_y.at[slot, tz],
            box_send.at[ty * 4 + tz],
            box_recv.at[slot * 4 + tz],
            "sec",
            mz * 4 + ty,
        )

    def along_z(tz, ty, slot):
        return remote(
            out_z.at[tz, ty],
            in_z.at[slot, ty],
            box_send.at[16 + tz * 4 + ty],
            box_recv.at[16 + slot * 4 + ty],
            "sec",
            tz * 4 + my,
        )

    def on_z(tz, slot):
        return remote(
            mid_out.at[0, tz],
            mid_in.at[0, slot],
            mid_send.at[tz],
            mid_recv.at[slot],
            "sec",
            tz * 4 + my,
        )

    def on_y(ty, slot):
        return remote(
            mid_out.at[1, ty],
            mid_in.at[1, slot],
            mid_send.at[4 + ty],
            mid_recv.at[4 + slot],
            "sec",
            mz * 4 + ty,
        )

    def pool(i, _):
        peers = [
            moved(me, *(pick(i, [step[one][axis] for step in ORDER]) for axis in range(2)))
            for one in range(2)
        ]
        hot = jnp.concatenate(
            [
                jnp.where(
                    lax.broadcasted_iota(jnp.int32, (TOKB, cells), 0)
                    == (gid_ref[...] - peer * TOKB),
                    1.0,
                    0.0,
                ).astype(BF16)
                for peer in peers
            ],
            axis=0,
        )
        both = dot(hot, enc[...]).astype(BF16)
        for one in range(2):
            tz, ty = peers[one] // 4, lax.rem(peers[one], 4)
            part = both[one * TOKB : (one + 1) * TOKB]
            near, far = part[:, :wide], part[:, wide:]

            @pl.when(ty != my)
            def _():
                out_y[ty, tz] = near
                along_y(ty, tz, my).start()

            @pl.when(ty == my)
            def _():
                in_y[my, tz] = near

            @pl.when(tz != mz)
            def _():
                out_z[tz, ty] = far
                along_z(tz, ty, mz).start()

            @pl.when(tz == mz)
            def _():
                in_z[mz, ty] = far

        return 0

    lax.fori_loop(0, n // 2, pool, 0)

    row = gid_ref[...]
    tok_hot = jnp.where(
        lax.broadcasted_iota(jnp.int32, (TOKB, cells), 0) == (row & (TOKB - 1)), 1.0, 0.0
    ).astype(BF16)
    cyc_hot = jnp.where(
        lax.broadcasted_iota(jnp.int32, (n, cells), 0) == (row >> 8), 1.0, 0.0
    ).astype(BF16)
    hist = dot_nt(cyc_hot, tok_hot)
    for r in range(n):
        cnt_out[r] = hist[r : r + 1, :]

    def send_counts(peer):
        remote(
            cnt_out.at[peer], cnt_in.at[me], cnt_send.at[peer], cnt_recv.at[me], "sec", peer
        ).start()

    each_peer(n, me, send_counts)
    cnt_in[me] = cnt_out[me]

    last = values.shape[1] - HEAD
    ones = jnp.where(
        lax.broadcasted_iota(jnp.int32, (last, values.shape[2]), 0) == 0, 1.0, 0.0
    ).astype(BF16)
    for c in range(values.shape[0]):
        values[c, HEAD:, :] = ones
    accs[...] = jnp.zeros_like(accs)

    def first_hop(j, _):
        ty, tz = lax.rem(my + j, 4), lax.rem(mz + j, 4)
        for other in range(4):
            along_y(ty, other, ty).wait()
            along_z(tz, other, tz).wait()
        return 0

    lax.fori_loop(1, 4, first_hop, 0)

    def added(ref, k):
        total = ref[0, k].astype(F32)
        for r in range(1, 4):
            total = total + ref[r, k].astype(F32)
        return total

    def second_hop(j, _):
        ty, tz = lax.rem(my + j, 4), lax.rem(mz + j, 4)
        mid_out[0, tz] = added(in_y, tz)
        on_z(tz, mz).start()
        mid_out[1, ty] = added(in_z, ty)
        on_y(ty, my).start()
        return 0

    lax.fori_loop(1, 4, second_hop, 0)
    mid_in[0, mz] = added(in_y, mz)
    mid_in[1, my] = added(in_z, my)

    def arrive(peer):
        remote(
            cnt_out.at[peer], cnt_in.at[peer], cnt_send.at[peer], cnt_recv.at[peer], "sec", peer
        ).wait()

    each_peer(n, me, arrive)

    def last_hop(j, _):
        ty, tz = lax.rem(my + j, 4), lax.rem(mz + j, 4)
        on_z(tz, tz).wait()
        on_y(ty, ty).wait()
        return 0

    lax.fori_loop(1, 4, last_hop, 0)
    counts = cnt_in[0]
    for r in range(1, n):
        counts = counts + cnt_in[r]
    halves = []
    for h in range(2):
        total = mid_in[h, 0]
        for r in range(1, 4):
            total = total + mid_in[h, r]
        halves.append(total)
    sums = jnp.concatenate(halves, axis=1)
    loads[2].wait()
    loads[3].wait()
    root = jnp.sqrt(jnp.transpose(jnp.broadcast_to(counts, (8, TOKB)))[:, 0:1] + 1.0)
    pooled = (sums / root).astype(BF16)
    lifted = dot(pooled, in_w[...])
    normed_ref[...] = (
        lifted * lax.rsqrt(jnp.mean(lifted * lifted, axis=-1, keepdims=True) + 1e-06)
    ).astype(BF16)

    low = low_lanes(TOKB)
    half = TOKB // 2
    planes = HEADS // 4

    def place(group, one, sign):
        dz, dy = (pick(group, [g[one][axis] for g in GROUPS]) for axis in range(2))
        return moved(me, sign * dz, sign * dy)

    def message(peer, slot):
        return remote(
            outmsg.at[peer], inmsg.at[slot], msg_send.at[peer], msg_recv.at[slot], "sec", peer
        )

    def send_group(group):
        for one in range(4):
            peer = place(group, one, 1)

            @pl.when(peer != me)
            def _():
                message(peer, me).start()

            @pl.when(peer == me)
            def _():
                inmsg[me] = outmsg[me]

    def sent_group(group):
        for one in range(4):
            peer = place(group, one, 1)

            @pl.when(peer != me)
            def _():
                message(peer, me).wait_send()

    def project(i, _):
        for j in range(2):
            group = lax.rem(me // 4 + planes + pick(i, [two[j] for two in PLANES]), planes)
            column = group * (4 * HEAD)
            q4, k4, v4 = (
                dot(
                    normed_ref[...],
                    qkv_w[:, pl.ds(pl.multiple_of(part * D + column, 4 * HEAD), 4 * HEAD)],
                )
                for part in range(3)
            )
            q4 = q4 * HEAD ** (-0.5)
            vt = jnp.transpose(v4).astype(BF16)
            for one in range(4):
                head = group * 4 + one
                lanes = slice(one // 2 * 128, one // 2 * 128 + 128)
                q, k = q4[:, lanes], k4[:, lanes]
                if one % 2 == 0:
                    packed = jnp.where(low, q, swap_halves(k))
                else:
                    packed = jnp.where(low, swap_halves(q), k)
                outmsg[head, 0:TOKB] = packed.astype(BF16)
                mine = vt[one * HEAD : (one + 1) * HEAD]
                outmsg[head, TOKB : TOKB + HEAD] = mine[:, :half]
                outmsg[head, TOKB + HEAD : TOKB + 2 * HEAD] = mine[:, half:]

        @pl.when(i == 0)
        def _():
            send_group(0)

        return 0

    lax.fori_loop(0, len(PLANES), project, 0)
    for group in range(1, WINDOW):
        send_group(group)

    def meet(q, k):
        acc = accs[q]
        for c in range(2):
            key = keys[k, c * 2 * TOKB : (c + 1) * 2 * TOKB]
            expo = jnp.exp2(dot_nt(key, queries[q]) * LOG2E).astype(BF16)
            acc = acc + dot(values[k * 2 + c], expo)
        accs[q] = acc

    def stage(i, _):
        @pl.when(i + WINDOW < planes)
        def _():
            sent_group(i)
            send_group(i + WINDOW)

        for one in range(4):
            peer = place(i, one, -1)

            @pl.when(peer != me)
            def _():
                message(peer, peer).wait_recv()

            span = slice(one * TOKB, (one + 1) * TOKB)
            qk = inmsg[peer, 0:TOKB]
            keys[i, span] = qk
            queries[i, span] = jnp.where(low, 0.0, swap_halves(qk.astype(F32))).astype(BF16)
            chunk = i * 2 + one // 2
            base = one % 2 * TOKB
            values[chunk, 0:HEAD, base : base + half] = inmsg[peer, TOKB : TOKB + HEAD]
            values[chunk, 0:HEAD, base + half : base + TOKB] = inmsg[
                peer, TOKB + HEAD : TOKB + 2 * HEAD
            ]

        def pair(t, _):
            fresh = t >= i
            q = jnp.where(fresh, i, t)
            meet(q, jnp.where(fresh, t - i, i))

            @pl.when((i == planes - 1) & ((t < i) | (t == 2 * i)))
            def _():
                acc = accs[q]
                ctx = (acc[:HEAD] / acc[HEAD : HEAD + 1]).astype(BF16)
                for one in range(4):
                    peer = place(q, one, -1)
                    mine = ctx[:, one * TOKB : (one + 1) * TOKB]

                    @pl.when(peer != me)
                    def _():
                        outctx[peer] = mine
                        remote(
                            outctx.at[peer],
                            inctx.at[me],
                            ctx_send.at[peer],
                            ctx_recv.at[me],
                            "sec",
                            peer,
                        ).start()

                    @pl.when(peer == me)
                    def _():
                        inctx[me] = mine

            return 0

        lax.fori_loop(0, 2 * i + 1, pair, 0)
        return 0

    lax.fori_loop(0, planes, stage, 0)

    for group in range(planes - WINDOW, planes):
        sent_group(group)

    def context(peer):
        remote(
            outctx.at[peer], inctx.at[peer], ctx_send.at[peer], ctx_recv.at[peer], "sec", peer
        ).wait()

    each_peer(n, me, context)
    for load in loads[4:]:
        load.wait()

    ctx = jnp.transpose(inctx[...].reshape(D, TOKB))
    mixed = (normed_ref[...].astype(F32) + dot(ctx, out_w[...])).astype(BF16)
    mixed_ref[...] = mixed
    term = cot_t[...].astype(F32) * jax.nn.sigmoid(dot_nt(den_t[...], mixed))
    part = lax.dot_general(
        term,
        mixed.astype(F32),
        (((1,), (0,)), ((), ())),
        precision=lax.Precision.HIGHEST,
        preferred_element_type=F32,
    )
    for p in range(n):
        c, h = p // 2, p % 2
        part_out[p] = part[h * 8 : h * 8 + 8, c * 128 : (c + 1) * 128]

    def send_part(peer):
        remote(
            part_out.at[peer], part_in.at[me], part_send.at[peer], part_recv.at[me], "sec", peer
        ).start()

    each_peer(n, me, send_part)
    part_in[me] = part_out[me]

    density = softplus(dot_nt(mixed, den_t[...]))
    blocks = vox.shape[0]
    for pair in range(HEIGHTS // 2):
        two = dot(mixed_ref[...], vox_w[:, pair * 256 : (pair + 1) * 256])
        vox[:, pair * 16 : pair * 16 + 16, :] = jnp.concatenate(
            [two[:, :128].reshape(blocks, 8, 128), two[:, 128:].reshape(blocks, 8, 128)], axis=1
        ).astype(BF16)
        for one in range(2):
            h = pair * 2 + one
            dens[:, h * 8 : h * 8 + 8, :] = jnp.broadcast_to(
                density[:, h : h + 1], (TOKB, 128)
            ).reshape(blocks, 8, 128)
    bundles = rays.shape[0] // 128
    owned = bundles // n
    factor = 4.0 / (n * KB * 128)

    def render(i, _):
        peer = lax.rem(me + i, n)
        for y in range(owned):
            bundle = peer * owned + y
            ray = rays[pl.ds(pl.multiple_of(bundle * 128, 128), 128), :]
            picks = [ids[j, bundle] for j in range(KB)]
            score = dot_nt(jnp.concatenate([vox[b] for b in picks], axis=0), ray)
            total = jnp.zeros((8, 128), F32)
            for j in range(KB):
                value = softplus(score[j * 128 : (j + 1) * 128]) * dens[picks[j]]
                total = total + jnp.sum(value.reshape(16, 8, 128), axis=0)
            tau_out[peer, y : y + 1, :] = jnp.sum(total, axis=0, keepdims=True) * factor

        @pl.when(i < n)
        def _():
            remote(
                tau_out.at[peer], tau_in.at[me], tau_send.at[peer], tau_recv.at[me], "sec", peer
            ).start()

        @pl.when(i == n)
        def _():
            tau_in[me] = tau_out[me]

        @pl.when(i == 3)
        def _():
            def wait_part(peer):
                remote(
                    part_out.at[peer],
                    part_in.at[peer],
                    part_send.at[peer],
                    part_recv.at[peer],
                    "sec",
                    peer,
                ).wait()

            each_peer(n, me, wait_part)
            row = part_in[0]
            for r in range(1, n):
                row = row + part_in[r]
            row_out[...] = row
            row_in[clip] = row

            def send_row(peer):
                remote(
                    row_out, row_in.at[clip], row_send.at[peer], row_recv.at[clip], "dp", peer
                ).start()

            each_peer(nd, clip, send_row)

        @pl.when(i == 8)
        def _():
            def wait_row(peer):
                remote(
                    row_out, row_in.at[peer], row_send.at[peer], row_recv.at[peer], "dp", peer
                ).wait()

            each_peer(nd, clip, wait_row)
            full = row_in[0]
            for r in range(1, nd):
                full = full + row_in[r]
            full_out[...] = full
            full_in[me] = full

            def send_full(peer):
                remote(
                    full_out, full_in.at[me], full_send.at[peer], full_recv.at[me], "sec", peer
                ).start()

            each_peer(n, me, send_full)

        return 0

    lax.fori_loop(1, n + 1, render, 0)

    def finish(peer):
        remote(
            full_out, full_in.at[peer], full_send.at[peer], full_recv.at[peer], "sec", peer
        ).wait()
        remote(
            tau_out.at[peer], tau_in.at[peer], tau_send.at[peer], tau_recv.at[peer], "sec", peer
        ).wait()

    each_peer(n, me, finish)


def finish_kernel(n, tau_ref, full_ref, depth_ref, grad_ref):
    for p in range(n):
        c, h = p // 2, p % 2
        grad_ref[h * 8 : h * 8 + 8, c * 128 : (c + 1) * 128] = full_ref[p]
    before = jnp.zeros(tau_ref.shape[1:], F32)
    depth = jnp.zeros(tau_ref.shape[1:], F32)
    for r in range(n):
        tau = tau_ref[r]
        depth = depth + (r + 0.5) * jnp.exp(-before) * (1.0 - jnp.exp(-tau))
        before = before + tau
    depth_ref[...] = depth


def any_space():
    return pl.BlockSpec(memory_space=pl.ANY)


def vmem():
    return pl.BlockSpec(memory_space=pltpu.VMEM)


def dma(count):
    return pltpu.SemaphoreType.DMA((count,))


def shards(
    range_features,
    conv_weight,
    cell_cycle,
    cell_token,
    in_weight,
    qkv_weight,
    out_weight,
    voxel_weight,
    density_weight,
    ray_embed,
    block_ids,
    density_cotangent,
):
    _, az_dev, beams, width = range_features.shape
    n, nd = lax.axis_size("sec"), lax.axis_size("dp")
    cells = az_dev * beams
    bundles = ray_embed.shape[0] // 128
    owned = bundles // n
    blocks = TOKB * HEIGHTS // 128
    message = (n, TOKB + TOKB // 2, 128)
    tau, full = pl.pallas_call(
        functools.partial(forecast_kernel, n, nd, cells, beams),
        out_shape=(
            jax.ShapeDtypeStruct((n, owned, 128), F32),
            jax.ShapeDtypeStruct((n, 8, 128), F32),
        ),
        in_specs=[pl.BlockSpec(memory_space=pltpu.SMEM)] + [vmem()] * 4 + [any_space()] * 7,
        out_specs=(vmem(), vmem()),
        scratch_shapes=[
            pltpu.VMEM((1, cells), jnp.int32),
            pltpu.VMEM((cells + 2 * beams, width), BF16),
            pltpu.VMEM((cells, width), BF16),
            pltpu.VMEM((4, 4, TOKB, width // 2), BF16),
            pltpu.VMEM((4, 4, TOKB, width // 2), BF16),
            pltpu.VMEM((4, 4, TOKB, width // 2), BF16),
            pltpu.VMEM((4, 4, TOKB, width // 2), BF16),
            pltpu.VMEM((2, 4, TOKB, width // 2), F32),
            pltpu.VMEM((2, 4, TOKB, width // 2), F32),
            pltpu.VMEM((n, 1, TOKB), F32),
            pltpu.VMEM((n, 1, TOKB), F32),
            pltpu.VMEM(message, BF16),
            pltpu.VMEM(message, BF16),
            pltpu.VMEM((TOKB, D), BF16),
            pltpu.VMEM((n // 4, 4 * TOKB, 128), BF16),
            pltpu.VMEM((n // 4, 4 * TOKB, 128), BF16),
            pltpu.VMEM((n // 2, HEAD + 16, 2 * TOKB), BF16),
            pltpu.VMEM((n // 4, HEAD + 16, 4 * TOKB), F32),
            pltpu.VMEM((n, HEAD, TOKB), BF16),
            pltpu.VMEM((n, HEAD, TOKB), BF16),
            pltpu.VMEM((TOKB, D), BF16),
            pltpu.VMEM((blocks, 128, EMB), BF16),
            pltpu.VMEM((blocks, 128, 128), F32),
            pltpu.VMEM((n, owned, 128), F32),
            pltpu.VMEM((n, 8, 128), F32),
            pltpu.VMEM((n, 8, 128), F32),
            pltpu.VMEM((8, 128), F32),
            pltpu.VMEM((nd, 8, 128), F32),
            pltpu.VMEM((8, 128), F32),
            pltpu.VMEM(conv_weight.shape, BF16),
            pltpu.VMEM(in_weight.shape, BF16),
            pltpu.VMEM(qkv_weight.shape, BF16),
            pltpu.VMEM(out_weight.shape, BF16),
            pltpu.VMEM(voxel_weight.shape, BF16),
            pltpu.VMEM(ray_embed.shape, BF16),
            dma(7),
            dma(2),
            dma(2),
            dma(32),
            dma(32),
            dma(8),
            dma(8),
            dma(n),
            dma(n),
            dma(n),
            dma(n),
            dma(n),
            dma(n),
            dma(n),
            dma(n),
            dma(n),
            dma(n),
            dma(nd),
            dma(nd),
            dma(n),
            dma(n),
        ],
        compiler_params=pltpu.CompilerParams(
            collective_id=0, has_side_effects=True, vmem_limit_bytes=VMEM_LIMIT
        ),
        name="forecast",
    )(
        block_ids[0].T,
        cell_cycle.reshape(az_dev, beams),
        cell_token,
        density_weight.T,
        density_cotangent[0].T,
        range_features.reshape(cells, width),
        conv_weight,
        in_weight,
        qkv_weight,
        out_weight,
        voxel_weight,
        ray_embed,
    )
    depth, grad = pl.pallas_call(
        functools.partial(finish_kernel, n),
        out_shape=(
            jax.ShapeDtypeStruct((owned, 128), F32),
            jax.ShapeDtypeStruct((HEIGHTS, D), F32),
        ),
        in_specs=[vmem(), vmem()],
        out_specs=(vmem(), vmem()),
        name="finish",
    )(tau, full)
    return depth.reshape(1, owned * 128), grad


def solution(mesh):
    placed = (
        P("dp", "sec", None, None),
        P(),
        P("sec", None, None),
        P("sec", None),
        P(),
        P(),
        P(),
        P(),
        P(),
        P(),
        P("sec", None, None),
        P("dp", "sec", None),
    )
    return jax.shard_map(
        shards, mesh=mesh, in_specs=placed, out_specs=(P("dp", "sec"), P()), check_vma=False
    )
```

```python
import functools
import math

import jax
import jax.numpy as jnp
from jax import lax
from jax.experimental import pallas as pl
from jax.experimental.pallas import tpu as pltpu
from jax.sharding import PartitionSpec as P

D = 1024
HEADS = 16
HEAD = 64
EMB = 128
KB = 4
TOKB = 256
HEIGHTS = 16
MESH = pl.DeviceIdType.MESH
BF16 = jnp.bfloat16
F32 = jnp.float32
VMEM_LIMIT = 60 * 1024 * 1024
LOG2E = math.log2(math.e)


def dot(a, b):
    return jnp.dot(a, b, preferred_element_type=F32)


def dot_nt(a, b):
    return lax.dot_general(a, b, (((1,), (1,)), ((), ())), preferred_element_type=F32)


def greet(axis, n):
    me = lax.axis_index(axis)
    barrier = pltpu.get_barrier_semaphore()

    def hello(i, _):
        pl.semaphore_signal(
            barrier, inc=1, device_id={axis: lax.rem(me + i, n)}, device_id_type=MESH
        )
        return 0

    lax.fori_loop(1, n, hello, 0)


def remote(src, dst, send_sem, recv_sem, axis, peer):
    return pltpu.make_async_remote_copy(
        src_ref=src,
        dst_ref=dst,
        send_sem=send_sem,
        recv_sem=recv_sem,
        device_id={axis: peer},
        device_id_type=MESH,
    )


def swap_halves(x):
    return pltpu.roll(x, HEAD, 1)


def low_lanes(rows):
    return lax.broadcasted_iota(jnp.int32, (rows, 128), 1) < HEAD


def pick(i, choices):
    chosen = jnp.int32(choices[0])
    for k, choice in enumerate(choices[1:]):
        chosen = jnp.where(i == k + 1, choice, chosen)
    return chosen


def moved(me, dz, dy):
    return lax.rem(me // 4 + dz + 4, 4) * 4 + lax.rem(me + dy + 4, 4)


ORDER = (
    ((1, 2), (-1, 2)),
    ((2, 1), (2, -1)),
    ((1, 1), (-1, -1)),
    ((1, -1), (-1, 1)),
    ((2, 0), (0, 2)),
    ((2, 2), (1, 0)),
    ((-1, 0), (0, 1)),
    ((0, -1), (0, 0)),
)
PLANES = ((1, -1), (2, 0))
GROUPS = (
    ((1, 1), (-1, -1), (1, -1), (-1, 1)),
    ((1, 2), (-1, 2), (2, 1), (2, -1)),
    ((2, 2), (2, 0), (0, 2), (0, 0)),
    ((1, 0), (-1, 0), (0, 1), (0, -1)),
)
WINDOW = 4


def each_peer(n, me, step):
    def body(i, _):
        step(lax.rem(me + n - i, n))
        return 0

    lax.fori_loop(1, n, body, 0)


def gelu(x):
    inner = math.sqrt(2.0 / math.pi) * (x + 0.044715 * (x * x * x))
    return x * (0.5 * (1.0 + jnp.tanh(inner)))


def softplus(x):
    return jnp.maximum(x, lax.log(1.0 + jnp.exp2(jnp.minimum(x, 80.0) * LOG2E)))


def forecast_kernel(
    n,
    nd,
    cells,
    beams,
    ids,
    cyc_ref,
    tok_ref,
    den_t,
    cot_t,
    feats,
    conv_hbm,
    in_hbm,
    qkv_hbm,
    out_hbm,
    vox_hbm,
    rays_hbm,
    tau_in,
    full_in,
    gid_ref,
    padded,
    enc,
    out_y,
    in_y,
    out_z,
    in_z,
    mid_out,
    mid_in,
    cnt_out,
    cnt_in,
    outmsg,
    inmsg,
    normed_ref,
    queries,
    keys,
    values,
    accs,
    outctx,
    inctx,
    mixed_ref,
    vox,
    dens,
    tau_out,
    part_out,
    part_in,
    row_out,
    row_in,
    full_out,
    conv_w,
    in_w,
    qkv_w,
    out_w,
    vox_w,
    rays,
    load_sem,
    halo_send,
    halo_recv,
    box_send,
    box_recv,
    mid_send,
    mid_recv,
    cnt_send,
    cnt_recv,
    msg_send,
    msg_recv,
    ctx_send,
    ctx_recv,
    tau_send,
    tau_recv,
    part_send,
    part_recv,
    row_send,
    row_recv,
    full_send,
    full_recv,
):
    me = lax.axis_index("sec")
    clip = lax.axis_index("dp")
    greet("sec", n)
    greet("dp", nd)
    loads = [
        pltpu.make_async_copy(feats, padded.at[pl.ds(beams, cells)], load_sem.at[0]),
        pltpu.make_async_copy(conv_hbm, conv_w, load_sem.at[1]),
        pltpu.make_async_copy(in_hbm, in_w, load_sem.at[2]),
        pltpu.make_async_copy(qkv_hbm, qkv_w, load_sem.at[3]),
        pltpu.make_async_copy(out_hbm, out_w, load_sem.at[4]),
        pltpu.make_async_copy(vox_hbm, vox_w, load_sem.at[5]),
        pltpu.make_async_copy(rays_hbm, rays, load_sem.at[6]),
    ]
    for load in loads[:2]:
        load.start()
    gid = cyc_ref[...] * TOKB + tok_ref[...]
    for p in range(cells // 128):
        gid_ref[0:1, p * 128 : (p + 1) * 128] = jnp.concatenate(
            [gid[2 * p : 2 * p + 1, :], gid[2 * p + 1 : 2 * p + 2, :]], axis=1
        )
    pl.semaphore_wait(pltpu.get_barrier_semaphore(), n - 1 + nd - 1)
    halos = [
        remote(
            feats.at[pl.ds(cells - beams, beams)],
            padded.at[pl.ds(0, beams)],
            halo_send.at[0],
            halo_recv.at[0],
            "sec",
            lax.rem(me + 1, n),
        ),
        remote(
            feats.at[pl.ds(0, beams)],
            padded.at[pl.ds(beams + cells, beams)],
            halo_send.at[1],
            halo_recv.at[1],
            "sec",
            lax.rem(me + n - 1, n),
        ),
    ]
    for halo in halos:
        halo.start()

    rows = 16 * beams
    chunks = cells // rows

    def encode_chunk(c):
        base = pl.multiple_of(c * rows, rows)
        total = jnp.zeros((rows, enc.shape[1]), F32)
        for k in range(3):
            total = total + dot(padded[pl.ds(base + k * beams, rows), :], conv_w[k])
        own = padded[pl.ds(base + beams, rows), :].astype(F32)
        enc[pl.ds(base, rows), :] = (own + gelu(total)).astype(BF16)

    loads[0].wait()
    loads[1].wait()
    for load in loads[2:]:
        load.start()

    def chunk(i, _):
        @pl.when(i == chunks - 2)
        def _():
            for halo in halos:
                halo.wait()

        encode_chunk(lax.rem(i + 1, chunks))
        return 0

    lax.fori_loop(0, chunks, chunk, 0)

    mz, my = me // 4, lax.rem(me, 4)
    wide = enc.shape[1] // 2

    def along_y(ty, tz, slot):
        return remote(
            out_y.at[ty, tz],
            in_y.at[slot, tz],
            box_send.at[ty * 4 + tz],
            box_recv.at[slot * 4 + tz],
            "sec",
            mz * 4 + ty,
        )

    def along_z(tz, ty, slot):
        return remote(
            out_z.at[tz, ty],
            in_z.at[slot, ty],
            box_send.at[16 + tz * 4 + ty],
            box_recv.at[16 + slot * 4 + ty],
            "sec",
            tz * 4 + my,
        )

    def on_z(tz, slot):
        return remote(
            mid_out.at[0, tz],
            mid_in.at[0, slot],
            mid_send.at[tz],
            mid_recv.at[slot],
            "sec",
            tz * 4 + my,
        )

    def on_y(ty, slot):
        return remote(
            mid_out.at[1, ty],
            mid_in.at[1, slot],
            mid_send.at[4 + ty],
            mid_recv.at[4 + slot],
            "sec",
            mz * 4 + ty,
        )

    def pool(i, _):
        peers = [
            moved(me, *(pick(i, [step[one][axis] for step in ORDER]) for axis in range(2)))
            for one in range(2)
        ]
        hot = jnp.concatenate(
            [
                jnp.where(
                    lax.broadcasted_iota(jnp.int32, (TOKB, cells), 0)
                    == (gid_ref[...] - peer * TOKB),
                    1.0,
                    0.0,
                ).astype(BF16)
                for peer in peers
            ],
            axis=0,
        )
        both = dot(hot, enc[...]).astype(BF16)
        for one in range(2):
            tz, ty = peers[one] // 4, lax.rem(peers[one], 4)
            part = both[one * TOKB : (one + 1) * TOKB]
            near, far = part[:, :wide], part[:, wide:]

            @pl.when(ty != my)
            def _():
                out_y[ty, tz] = near
                along_y(ty, tz, my).start()

            @pl.when(ty == my)
            def _():
                in_y[my, tz] = near

            @pl.when(tz != mz)
            def _():
                out_z[tz, ty] = far
                along_z(tz, ty, mz).start()

            @pl.when(tz == mz)
            def _():
                in_z[mz, ty] = far

        return 0

    lax.fori_loop(0, n // 2, pool, 0)

    row = gid_ref[...]
    tok_hot = jnp.where(
        lax.broadcasted_iota(jnp.int32, (TOKB, cells), 0) == (row & (TOKB - 1)), 1.0, 0.0
    ).astype(BF16)
    cyc_hot = jnp.where(
        lax.broadcasted_iota(jnp.int32, (n, cells), 0) == (row >> 8), 1.0, 0.0
    ).astype(BF16)
    hist = dot_nt(cyc_hot, tok_hot)
    for r in range(n):
        cnt_out[r] = hist[r : r + 1, :]

    def send_counts(peer):
        remote(
            cnt_out.at[peer], cnt_in.at[me], cnt_send.at[peer], cnt_recv.at[me], "sec", peer
        ).start()

    each_peer(n, me, send_counts)
    cnt_in[me] = cnt_out[me]

    last = values.shape[1] - HEAD
    ones = jnp.where(
        lax.broadcasted_iota(jnp.int32, (last, values.shape[2]), 0) == 0, 1.0, 0.0
    ).astype(BF16)
    for c in range(values.shape[0]):
        values[c, HEAD:, :] = ones
    accs[...] = jnp.zeros_like(accs)

    def first_hop(j, _):
        ty, tz = lax.rem(my + j, 4), lax.rem(mz + j, 4)
        for other in range(4):
            along_y(ty, other, ty).wait()
            along_z(tz, other, tz).wait()
        return 0

    lax.fori_loop(1, 4, first_hop, 0)

    def added(ref, k):
        total = ref[0, k].astype(F32)
        for r in range(1, 4):
            total = total + ref[r, k].astype(F32)
        return total

    def second_hop(j, _):
        ty, tz = lax.rem(my + j, 4), lax.rem(mz + j, 4)
        mid_out[0, tz] = added(in_y, tz)
        on_z(tz, mz).start()
        mid_out[1, ty] = added(in_z, ty)
        on_y(ty, my).start()
        return 0

    lax.fori_loop(1, 4, second_hop, 0)
    mid_in[0, mz] = added(in_y, mz)
    mid_in[1, my] = added(in_z, my)

    def arrive(peer):
        remote(
            cnt_out.at[peer], cnt_in.at[peer], cnt_send.at[peer], cnt_recv.at[peer], "sec", peer
        ).wait()

    each_peer(n, me, arrive)

    def last_hop(j, _):
        ty, tz = lax.rem(my + j, 4), lax.rem(mz + j, 4)
        on_z(tz, tz).wait()
        on_y(ty, ty).wait()
        return 0

    lax.fori_loop(1, 4, last_hop, 0)
    counts = cnt_in[0]
    for r in range(1, n):
        counts = counts + cnt_in[r]
    halves = []
    for h in range(2):
        total = mid_in[h, 0]
        for r in range(1, 4):
            total = total + mid_in[h, r]
        halves.append(total)
    sums = jnp.concatenate(halves, axis=1)
    loads[2].wait()
    loads[3].wait()
    root = jnp.sqrt(jnp.transpose(jnp.broadcast_to(counts, (8, TOKB)))[:, 0:1] + 1.0)
    pooled = (sums / root).astype(BF16)
    lifted = dot(pooled, in_w[...])
    normed_ref[...] = (
        lifted * lax.rsqrt(jnp.mean(lifted * lifted, axis=-1, keepdims=True) + 1e-06)
    ).astype(BF16)

    low = low_lanes(TOKB)
    half = TOKB // 2
    planes = HEADS // 4

    def place(group, one, sign):
        dz, dy = (pick(group, [g[one][axis] for g in GROUPS]) for axis in range(2))
        return moved(me, sign * dz, sign * dy)

    def message(peer, slot):
        return remote(
            outmsg.at[peer], inmsg.at[slot], msg_send.at[peer], msg_recv.at[slot], "sec", peer
        )

    def send_group(group):
        for one in range(4):
            peer = place(group, one, 1)

            @pl.when(peer != me)
            def _():
                message(peer, me).start()

            @pl.when(peer == me)
            def _():
                inmsg[me] = outmsg[me]

    def sent_group(group):
        for one in range(4):
            peer = place(group, one, 1)

            @pl.when(peer != me)
            def _():
                message(peer, me).wait_send()

    def project(i, _):
        for j in range(2):
            group = lax.rem(me // 4 + planes + pick(i, [two[j] for two in PLANES]), planes)
            column = group * (4 * HEAD)
            q4, k4, v4 = (
                dot(
                    normed_ref[...],
                    qkv_w[:, pl.ds(pl.multiple_of(part * D + column, 4 * HEAD), 4 * HEAD)],
                )
                for part in range(3)
            )
            q4 = q4 * HEAD ** (-0.5)
            vt = jnp.transpose(v4).astype(BF16)
            for one in range(4):
                head = group * 4 + one
                lanes = slice(one // 2 * 128, one // 2 * 128 + 128)
                q, k = q4[:, lanes], k4[:, lanes]
                if one % 2 == 0:
                    packed = jnp.where(low, q, swap_halves(k))
                else:
                    packed = jnp.where(low, swap_halves(q), k)
                outmsg[head, 0:TOKB] = packed.astype(BF16)
                mine = vt[one * HEAD : (one + 1) * HEAD]
                outmsg[head, TOKB : TOKB + HEAD] = mine[:, :half]
                outmsg[head, TOKB + HEAD : TOKB + 2 * HEAD] = mine[:, half:]

        @pl.when(i == 0)
        def _():
            send_group(0)

        return 0

    lax.fori_loop(0, len(PLANES), project, 0)
    for group in range(1, WINDOW):
        send_group(group)

    def meet(q, k):
        acc = accs[q]
        for c in range(2):
            key = keys[k, c * 2 * TOKB : (c + 1) * 2 * TOKB]
            expo = jnp.exp2(dot_nt(key, queries[q]) * LOG2E).astype(BF16)
            acc = acc + dot(values[k * 2 + c], expo)
        accs[q] = acc

    def stage(i, _):
        @pl.when(i + WINDOW < planes)
        def _():
            sent_group(i)
            send_group(i + WINDOW)

        for one in range(4):
            peer = place(i, one, -1)

            @pl.when(peer != me)
            def _():
                message(peer, peer).wait_recv()

            span = slice(one * TOKB, (one + 1) * TOKB)
            qk = inmsg[peer, 0:TOKB]
            keys[i, span] = qk
            queries[i, span] = jnp.where(low, 0.0, swap_halves(qk.astype(F32))).astype(BF16)
            chunk = i * 2 + one // 2
            base = one % 2 * TOKB
            values[chunk, 0:HEAD, base : base + half] = inmsg[peer, TOKB : TOKB + HEAD]
            values[chunk, 0:HEAD, base + half : base + TOKB] = inmsg[
                peer, TOKB + HEAD : TOKB + 2 * HEAD
            ]

        def pair(t, _):
            fresh = t >= i
            q = jnp.where(fresh, i, t)
            meet(q, jnp.where(fresh, t - i, i))

            @pl.when((i == planes - 1) & ((t < i) | (t == 2 * i)))
            def _():
                acc = accs[q]
                ctx = (acc[:HEAD] / acc[HEAD : HEAD + 1]).astype(BF16)
                for one in range(4):
                    peer = place(q, one, -1)
                    mine = ctx[:, one * TOKB : (one + 1) * TOKB]

                    @pl.when(peer != me)
                    def _():
                        outctx[peer] = mine
                        remote(
                            outctx.at[peer],
                            inctx.at[me],
                            ctx_send.at[peer],
                            ctx_recv.at[me],
                            "sec",
                            peer,
                        ).start()

                    @pl.when(peer == me)
                    def _():
                        inctx[me] = mine

            return 0

        lax.fori_loop(0, 2 * i + 1, pair, 0)
        return 0

    lax.fori_loop(0, planes, stage, 0)

    for group in range(planes - WINDOW, planes):
        sent_group(group)

    def context(peer):
        remote(
            outctx.at[peer], inctx.at[peer], ctx_send.at[peer], ctx_recv.at[peer], "sec", peer
        ).wait()

    each_peer(n, me, context)
    for load in loads[4:]:
        load.wait()

    ctx = jnp.transpose(inctx[...].reshape(D, TOKB))
    mixed = (normed_ref[...].astype(F32) + dot(ctx, out_w[...])).astype(BF16)
    mixed_ref[...] = mixed
    term = cot_t[...].astype(F32) * jax.nn.sigmoid(dot_nt(den_t[...], mixed))
    part = lax.dot_general(
        term,
        mixed.astype(F32),
        (((1,), (0,)), ((), ())),
        precision=lax.Precision.HIGHEST,
        preferred_element_type=F32,
    )
    for p in range(n):
        c, h = p // 2, p % 2
        part_out[p] = part[h * 8 : h * 8 + 8, c * 128 : (c + 1) * 128]

    def send_part(peer):
        remote(
            part_out.at[peer], part_in.at[me], part_send.at[peer], part_recv.at[me], "sec", peer
        ).start()

    each_peer(n, me, send_part)
    part_in[me] = part_out[me]

    density = softplus(dot_nt(mixed, den_t[...]))
    blocks = vox.shape[0]
    for pair in range(HEIGHTS // 2):
        two = dot(mixed_ref[...], vox_w[:, pair * 256 : (pair + 1) * 256])
        vox[:, pair * 16 : pair * 16 + 16, :] = jnp.concatenate(
            [two[:, :128].reshape(blocks, 8, 128), two[:, 128:].reshape(blocks, 8, 128)], axis=1
        ).astype(BF16)
        for one in range(2):
            h = pair * 2 + one
            dens[:, h * 8 : h * 8 + 8, :] = jnp.broadcast_to(
                density[:, h : h + 1], (TOKB, 128)
            ).reshape(blocks, 8, 128)
    bundles = rays.shape[0] // 128
    owned = bundles // n
    factor = 4.0 / (n * KB * 128)

    def render(i, _):
        peers = [lax.rem(me + 2 * i + 1 + one, n) for one in range(2)]
        for peer in peers:
            for y in range(owned):
                bundle = peer * owned + y
                ray = rays[pl.ds(pl.multiple_of(bundle * 128, 128), 128), :]
                picks = [ids[j, bundle] for j in range(KB)]
                score = dot_nt(jnp.concatenate([vox[b] for b in picks], axis=0), ray)
                total = jnp.zeros((8, 128), F32)
                for j in range(KB):
                    value = softplus(score[j * 128 : (j + 1) * 128]) * dens[picks[j]]
                    total = total + jnp.sum(value.reshape(16, 8, 128), axis=0)
                tau_out[peer, y : y + 1, :] = jnp.sum(total, axis=0, keepdims=True) * factor

        for peer in peers:

            @pl.when(peer != me)
            def _():
                remote(
                    tau_out.at[peer], tau_in.at[me], tau_send.at[peer], tau_recv.at[me], "sec", peer
                ).start()

            @pl.when(peer == me)
            def _():
                tau_in[me] = tau_out[me]

        @pl.when(i == 1)
        def _():
            def wait_part(peer):
                remote(
                    part_out.at[peer],
                    part_in.at[peer],
                    part_send.at[peer],
                    part_recv.at[peer],
                    "sec",
                    peer,
                ).wait()

            each_peer(n, me, wait_part)
            row = part_in[0]
            for r in range(1, n):
                row = row + part_in[r]
            row_out[...] = row
            row_in[clip] = row

            def send_row(peer):
                remote(
                    row_out, row_in.at[clip], row_send.at[peer], row_recv.at[clip], "dp", peer
                ).start()

            each_peer(nd, clip, send_row)

        @pl.when(i == 4)
        def _():
            def wait_row(peer):
                remote(
                    row_out, row_in.at[peer], row_send.at[peer], row_recv.at[peer], "dp", peer
                ).wait()

            each_peer(nd, clip, wait_row)
            full = row_in[0]
            for r in range(1, nd):
                full = full + row_in[r]
            full_out[...] = full
            full_in[me] = full

            def send_full(peer):
                remote(
                    full_out, full_in.at[me], full_send.at[peer], full_recv.at[me], "sec", peer
                ).start()

            each_peer(n, me, send_full)

        return 0

    lax.fori_loop(0, n // 2, render, 0)

    def finish(peer):
        remote(
            full_out, full_in.at[peer], full_send.at[peer], full_recv.at[peer], "sec", peer
        ).wait()
        remote(
            tau_out.at[peer], tau_in.at[peer], tau_send.at[peer], tau_recv.at[peer], "sec", peer
        ).wait()

    each_peer(n, me, finish)


def finish_kernel(n, tau_ref, full_ref, depth_ref, grad_ref):
    for p in range(n):
        c, h = p // 2, p % 2
        grad_ref[h * 8 : h * 8 + 8, c * 128 : (c + 1) * 128] = full_ref[p]
    before = jnp.zeros(tau_ref.shape[1:], F32)
    depth = jnp.zeros(tau_ref.shape[1:], F32)
    for r in range(n):
        tau = tau_ref[r]
        depth = depth + (r + 0.5) * jnp.exp(-before) * (1.0 - jnp.exp(-tau))
        before = before + tau
    depth_ref[...] = depth


def any_space():
    return pl.BlockSpec(memory_space=pl.ANY)


def vmem():
    return pl.BlockSpec(memory_space=pltpu.VMEM)


def dma(count):
    return pltpu.SemaphoreType.DMA((count,))


def shards(
    range_features,
    conv_weight,
    cell_cycle,
    cell_token,
    in_weight,
    qkv_weight,
    out_weight,
    voxel_weight,
    density_weight,
    ray_embed,
    block_ids,
    density_cotangent,
):
    _, az_dev, beams, width = range_features.shape
    n, nd = lax.axis_size("sec"), lax.axis_size("dp")
    cells = az_dev * beams
    bundles = ray_embed.shape[0] // 128
    owned = bundles // n
    blocks = TOKB * HEIGHTS // 128
    message = (n, TOKB + TOKB // 2, 128)
    tau, full = pl.pallas_call(
        functools.partial(forecast_kernel, n, nd, cells, beams),
        out_shape=(
            jax.ShapeDtypeStruct((n, owned, 128), F32),
            jax.ShapeDtypeStruct((n, 8, 128), F32),
        ),
        in_specs=[pl.BlockSpec(memory_space=pltpu.SMEM)] + [vmem()] * 4 + [any_space()] * 7,
        out_specs=(vmem(), vmem()),
        scratch_shapes=[
            pltpu.VMEM((1, cells), jnp.int32),
            pltpu.VMEM((cells + 2 * beams, width), BF16),
            pltpu.VMEM((cells, width), BF16),
            pltpu.VMEM((4, 4, TOKB, width // 2), BF16),
            pltpu.VMEM((4, 4, TOKB, width // 2), BF16),
            pltpu.VMEM((4, 4, TOKB, width // 2), BF16),
            pltpu.VMEM((4, 4, TOKB, width // 2), BF16),
            pltpu.VMEM((2, 4, TOKB, width // 2), F32),
            pltpu.VMEM((2, 4, TOKB, width // 2), F32),
            pltpu.VMEM((n, 1, TOKB), F32),
            pltpu.VMEM((n, 1, TOKB), F32),
            pltpu.VMEM(message, BF16),
            pltpu.VMEM(message, BF16),
            pltpu.VMEM((TOKB, D), BF16),
            pltpu.VMEM((n // 4, 4 * TOKB, 128), BF16),
            pltpu.VMEM((n // 4, 4 * TOKB, 128), BF16),
            pltpu.VMEM((n // 2, HEAD + 16, 2 * TOKB), BF16),
            pltpu.VMEM((n // 4, HEAD + 16, 4 * TOKB), F32),
            pltpu.VMEM((n, HEAD, TOKB), BF16),
            pltpu.VMEM((n, HEAD, TOKB), BF16),
            pltpu.VMEM((TOKB, D), BF16),
            pltpu.VMEM((blocks, 128, EMB), BF16),
            pltpu.VMEM((blocks, 128, 128), F32),
            pltpu.VMEM((n, owned, 128), F32),
            pltpu.VMEM((n, 8, 128), F32),
            pltpu.VMEM((n, 8, 128), F32),
            pltpu.VMEM((8, 128), F32),
            pltpu.VMEM((nd, 8, 128), F32),
            pltpu.VMEM((8, 128), F32),
            pltpu.VMEM(conv_weight.shape, BF16),
            pltpu.VMEM(in_weight.shape, BF16),
            pltpu.VMEM(qkv_weight.shape, BF16),
            pltpu.VMEM(out_weight.shape, BF16),
            pltpu.VMEM(voxel_weight.shape, BF16),
            pltpu.VMEM(ray_embed.shape, BF16),
            dma(7),
            dma(2),
            dma(2),
            dma(32),
            dma(32),
            dma(8),
            dma(8),
            dma(n),
            dma(n),
            dma(n),
            dma(n),
            dma(n),
            dma(n),
            dma(n),
            dma(n),
            dma(n),
            dma(n),
            dma(nd),
            dma(nd),
            dma(n),
            dma(n),
        ],
        compiler_params=pltpu.CompilerParams(
            collective_id=0, has_side_effects=True, vmem_limit_bytes=VMEM_LIMIT
        ),
        name="forecast",
    )(
        block_ids[0].T,
        cell_cycle.reshape(az_dev, beams),
        cell_token,
        density_weight.T,
        density_cotangent[0].T,
        range_features.reshape(cells, width),
        conv_weight,
        in_weight,
        qkv_weight,
        out_weight,
        voxel_weight,
        ray_embed,
    )
    depth, grad = pl.pallas_call(
        functools.partial(finish_kernel, n),
        out_shape=(
            jax.ShapeDtypeStruct((owned, 128), F32),
            jax.ShapeDtypeStruct((HEIGHTS, D), F32),
        ),
        in_specs=[vmem(), vmem()],
        out_specs=(vmem(), vmem()),
        name="finish",
    )(tau, full)
    return depth.reshape(1, owned * 128), grad


def solution(mesh):
    placed = (
        P("dp", "sec", None, None),
        P(),
        P("sec", None, None),
        P("sec", None),
        P(),
        P(),
        P(),
        P(),
        P(),
        P(),
        P("sec", None, None),
        P("dp", "sec", None),
    )
    return jax.shard_map(
        shards, mesh=mesh, in_specs=placed, out_specs=(P("dp", "sec"), P()), check_vma=False
    )
```

```python
import functools
import math

import jax
import jax.numpy as jnp
from jax import lax
from jax.experimental import pallas as pl
from jax.experimental.pallas import tpu as pltpu
from jax.sharding import PartitionSpec as P

D = 1024
HEADS = 16
HEAD = 64
EMB = 128
KB = 4
TOKB = 256
HEIGHTS = 16
MESH = pl.DeviceIdType.MESH
BF16 = jnp.bfloat16
F32 = jnp.float32
VMEM_LIMIT = 60 * 1024 * 1024
LOG2E = math.log2(math.e)


def dot(a, b):
    return jnp.dot(a, b, preferred_element_type=F32)


def dot_nt(a, b):
    return lax.dot_general(a, b, (((1,), (1,)), ((), ())), preferred_element_type=F32)


def greet(axis, n):
    me = lax.axis_index(axis)
    barrier = pltpu.get_barrier_semaphore()

    def hello(i, _):
        pl.semaphore_signal(
            barrier, inc=1, device_id={axis: lax.rem(me + i, n)}, device_id_type=MESH
        )
        return 0

    lax.fori_loop(1, n, hello, 0)


def remote(src, dst, send_sem, recv_sem, axis, peer):
    return pltpu.make_async_remote_copy(
        src_ref=src,
        dst_ref=dst,
        send_sem=send_sem,
        recv_sem=recv_sem,
        device_id={axis: peer},
        device_id_type=MESH,
    )


def swap_halves(x):
    return pltpu.roll(x, HEAD, 1)


def low_lanes(rows):
    return lax.broadcasted_iota(jnp.int32, (rows, 128), 1) < HEAD


def pick(i, choices):
    chosen = jnp.int32(choices[0])
    for k, choice in enumerate(choices[1:]):
        chosen = jnp.where(i == k + 1, choice, chosen)
    return chosen


def moved(me, dz, dy):
    return lax.rem(me // 4 + dz + 4, 4) * 4 + lax.rem(me + dy + 4, 4)


ORDER = (
    ((1, 2), (-1, 2)),
    ((2, 1), (2, -1)),
    ((1, 1), (-1, -1)),
    ((1, -1), (-1, 1)),
    ((2, 0), (0, 2)),
    ((2, 2), (1, 0)),
    ((-1, 0), (0, 1)),
    ((0, -1), (0, 0)),
)
PLANES = ((1, -1), (2, 0))
GROUPS = (
    ((1, 1), (-1, -1), (1, -1), (-1, 1)),
    ((1, 2), (-1, 2), (2, 1), (2, -1)),
    ((2, 2), (2, 0), (0, 2), (0, 0)),
    ((1, 0), (-1, 0), (0, 1), (0, -1)),
)
WINDOW = 4


def each_peer(n, me, step):
    def body(i, _):
        step(lax.rem(me + n - i, n))
        return 0

    lax.fori_loop(1, n, body, 0)


def gelu(x):
    inner = math.sqrt(2.0 / math.pi) * (x + 0.044715 * (x * x * x))
    return x * (0.5 * (1.0 + jnp.tanh(inner)))


def softplus(x):
    return jnp.maximum(x, lax.log(1.0 + jnp.exp2(jnp.minimum(x, 80.0) * LOG2E)))


def forecast_kernel(
    n,
    nd,
    cells,
    beams,
    ids,
    cyc_ref,
    tok_ref,
    den_t,
    cot_t,
    feats,
    conv_hbm,
    in_hbm,
    qkv_hbm,
    out_hbm,
    vox_hbm,
    rays_hbm,
    tau_in,
    full_in,
    gid_ref,
    padded,
    enc,
    out_y,
    in_y,
    out_z,
    in_z,
    mid_out,
    mid_in,
    cnt_out,
    cnt_in,
    outmsg,
    inmsg,
    normed_ref,
    queries,
    keys,
    values,
    accs,
    outctx,
    inctx,
    mixed_ref,
    vox,
    dens,
    tau_out,
    part_out,
    part_in,
    row_out,
    row_in,
    full_out,
    conv_w,
    in_w,
    qkv_w,
    out_w,
    vox_w,
    rays,
    load_sem,
    halo_send,
    halo_recv,
    box_send,
    box_recv,
    mid_send,
    mid_recv,
    cnt_send,
    cnt_recv,
    msg_send,
    msg_recv,
    ctx_send,
    ctx_recv,
    tau_send,
    tau_recv,
    part_send,
    part_recv,
    row_send,
    row_recv,
    full_send,
    full_recv,
):
    me = lax.axis_index("sec")
    clip = lax.axis_index("dp")
    greet("sec", n)
    greet("dp", nd)
    loads = [
        pltpu.make_async_copy(feats, padded.at[pl.ds(beams, cells)], load_sem.at[0]),
        pltpu.make_async_copy(conv_hbm, conv_w, load_sem.at[1]),
        pltpu.make_async_copy(in_hbm, in_w, load_sem.at[2]),
        pltpu.make_async_copy(qkv_hbm, qkv_w, load_sem.at[3]),
        pltpu.make_async_copy(out_hbm, out_w, load_sem.at[4]),
        pltpu.make_async_copy(vox_hbm, vox_w, load_sem.at[5]),
        pltpu.make_async_copy(rays_hbm, rays, load_sem.at[6]),
    ]
    for load in loads[:2]:
        load.start()
    gid = cyc_ref[...] * TOKB + tok_ref[...]
    for p in range(cells // 128):
        gid_ref[0:1, p * 128 : (p + 1) * 128] = jnp.concatenate(
            [gid[2 * p : 2 * p + 1, :], gid[2 * p + 1 : 2 * p + 2, :]], axis=1
        )
    pl.semaphore_wait(pltpu.get_barrier_semaphore(), n - 1 + nd - 1)
    halos = [
        remote(
            feats.at[pl.ds(cells - beams, beams)],
            padded.at[pl.ds(0, beams)],
            halo_send.at[0],
            halo_recv.at[0],
            "sec",
            lax.rem(me + 1, n),
        ),
        remote(
            feats.at[pl.ds(0, beams)],
            padded.at[pl.ds(beams + cells, beams)],
            halo_send.at[1],
            halo_recv.at[1],
            "sec",
            lax.rem(me + n - 1, n),
        ),
    ]
    for halo in halos:
        halo.start()

    rows = 16 * beams
    chunks = cells // rows

    def encode_chunk(c):
        base = pl.multiple_of(c * rows, rows)
        total = jnp.zeros((rows, enc.shape[1]), F32)
        for k in range(3):
            total = total + dot(padded[pl.ds(base + k * beams, rows), :], conv_w[k])
        own = padded[pl.ds(base + beams, rows), :].astype(F32)
        enc[pl.ds(base, rows), :] = (own + gelu(total)).astype(BF16)

    loads[0].wait()
    loads[1].wait()
    for load in loads[2:]:
        load.start()

    def chunk(i, _):
        @pl.when(i == chunks - 2)
        def _():
            for halo in halos:
                halo.wait()

        encode_chunk(lax.rem(i + 1, chunks))
        return 0

    lax.fori_loop(0, chunks, chunk, 0)

    mz, my = me // 4, lax.rem(me, 4)
    wide = enc.shape[1] // 2

    def along_y(ty, tz, slot):
        return remote(
            out_y.at[ty, tz],
            in_y.at[slot, tz],
            box_send.at[ty * 4 + tz],
            box_recv.at[slot * 4 + tz],
            "sec",
            mz * 4 + ty,
        )

    def along_z(tz, ty, slot):
        return remote(
            out_z.at[tz, ty],
            in_z.at[slot, ty],
            box_send.at[16 + tz * 4 + ty],
            box_recv.at[16 + slot * 4 + ty],
            "sec",
            tz * 4 + my,
        )

    def on_z(tz, slot):
        return remote(
            mid_out.at[0, tz],
            mid_in.at[0, slot],
            mid_send.at[tz],
            mid_recv.at[slot],
            "sec",
            tz * 4 + my,
        )

    def on_y(ty, slot):
        return remote(
            mid_out.at[1, ty],
            mid_in.at[1, slot],
            mid_send.at[4 + ty],
            mid_recv.at[4 + slot],
            "sec",
            mz * 4 + ty,
        )

    def pool(i, _):
        peers = [
            moved(me, *(pick(i, [step[one][axis] for step in ORDER]) for axis in range(2)))
            for one in range(2)
        ]
        hot = jnp.concatenate(
            [
                jnp.where(
                    lax.broadcasted_iota(jnp.int32, (TOKB, cells), 0)
                    == (gid_ref[...] - peer * TOKB),
                    1.0,
                    0.0,
                ).astype(BF16)
                for peer in peers
            ],
            axis=0,
        )
        both = dot(hot, enc[...]).astype(BF16)
        for one in range(2):
            tz, ty = peers[one] // 4, lax.rem(peers[one], 4)
            part = both[one * TOKB : (one + 1) * TOKB]
            near, far = part[:, :wide], part[:, wide:]

            @pl.when(ty != my)
            def _():
                out_y[ty, tz] = near
                along_y(ty, tz, my).start()

            @pl.when(ty == my)
            def _():
                in_y[my, tz] = near

            @pl.when(tz != mz)
            def _():
                out_z[tz, ty] = far
                along_z(tz, ty, mz).start()

            @pl.when(tz == mz)
            def _():
                in_z[mz, ty] = far

        return 0

    lax.fori_loop(0, n // 2, pool, 0)

    row = gid_ref[...]
    tok_hot = jnp.where(
        lax.broadcasted_iota(jnp.int32, (TOKB, cells), 0) == (row & (TOKB - 1)), 1.0, 0.0
    ).astype(BF16)
    cyc_hot = jnp.where(
        lax.broadcasted_iota(jnp.int32, (n, cells), 0) == (row >> 8), 1.0, 0.0
    ).astype(BF16)
    hist = dot_nt(cyc_hot, tok_hot)
    for r in range(n):
        cnt_out[r] = hist[r : r + 1, :]

    def send_counts(peer):
        remote(
            cnt_out.at[peer], cnt_in.at[me], cnt_send.at[peer], cnt_recv.at[me], "sec", peer
        ).start()

    each_peer(n, me, send_counts)
    cnt_in[me] = cnt_out[me]

    last = values.shape[1] - HEAD
    ones = jnp.where(
        lax.broadcasted_iota(jnp.int32, (last, values.shape[2]), 0) == 0, 1.0, 0.0
    ).astype(BF16)
    for c in range(values.shape[0]):
        values[c, HEAD:, :] = ones
    accs[...] = jnp.zeros_like(accs)

    def first_hop(j, _):
        ty, tz = lax.rem(my + j, 4), lax.rem(mz + j, 4)
        for other in range(4):
            along_y(ty, other, ty).wait()
            along_z(tz, other, tz).wait()
        return 0

    lax.fori_loop(1, 4, first_hop, 0)

    def added(ref, k):
        total = ref[0, k].astype(F32)
        for r in range(1, 4):
            total = total + ref[r, k].astype(F32)
        return total

    def second_hop(j, _):
        ty, tz = lax.rem(my + j, 4), lax.rem(mz + j, 4)
        mid_out[0, tz] = added(in_y, tz)
        on_z(tz, mz).start()
        mid_out[1, ty] = added(in_z, ty)
        on_y(ty, my).start()
        return 0

    lax.fori_loop(1, 4, second_hop, 0)
    mid_in[0, mz] = added(in_y, mz)
    mid_in[1, my] = added(in_z, my)

    def arrive(peer):
        remote(
            cnt_out.at[peer], cnt_in.at[peer], cnt_send.at[peer], cnt_recv.at[peer], "sec", peer
        ).wait()

    each_peer(n, me, arrive)

    def last_hop(j, _):
        ty, tz = lax.rem(my + j, 4), lax.rem(mz + j, 4)
        on_z(tz, tz).wait()
        on_y(ty, ty).wait()
        return 0

    lax.fori_loop(1, 4, last_hop, 0)
    counts = cnt_in[0]
    for r in range(1, n):
        counts = counts + cnt_in[r]
    halves = []
    for h in range(2):
        total = mid_in[h, 0]
        for r in range(1, 4):
            total = total + mid_in[h, r]
        halves.append(total)
    sums = jnp.concatenate(halves, axis=1)
    loads[2].wait()
    loads[3].wait()
    root = jnp.sqrt(jnp.transpose(jnp.broadcast_to(counts, (8, TOKB)))[:, 0:1] + 1.0)
    pooled = (sums / root).astype(BF16)
    lifted = dot(pooled, in_w[...])
    normed_ref[...] = (
        lifted * lax.rsqrt(jnp.mean(lifted * lifted, axis=-1, keepdims=True) + 1e-06)
    ).astype(BF16)

    low = low_lanes(TOKB)
    half = TOKB // 2
    planes = HEADS // 4

    def place(group, one, sign):
        dz, dy = (pick(group, [g[one][axis] for g in GROUPS]) for axis in range(2))
        return moved(me, sign * dz, sign * dy)

    def message(peer, slot):
        return remote(
            outmsg.at[peer], inmsg.at[slot], msg_send.at[peer], msg_recv.at[slot], "sec", peer
        )

    def send_group(group):
        for one in range(4):
            peer = place(group, one, 1)

            @pl.when(peer != me)
            def _():
                message(peer, me).start()

            @pl.when(peer == me)
            def _():
                inmsg[me] = outmsg[me]

    def sent_group(group):
        for one in range(4):
            peer = place(group, one, 1)

            @pl.when(peer != me)
            def _():
                message(peer, me).wait_send()

    def project(i, _):
        for j in range(2):
            group = lax.rem(me // 4 + planes + pick(i, [two[j] for two in PLANES]), planes)
            column = group * (4 * HEAD)
            q4, k4, v4 = (
                dot(
                    normed_ref[...],
                    qkv_w[:, pl.ds(pl.multiple_of(part * D + column, 4 * HEAD), 4 * HEAD)],
                )
                for part in range(3)
            )
            q4 = q4 * HEAD ** (-0.5)
            vt = jnp.transpose(v4).astype(BF16)
            for one in range(4):
                head = group * 4 + one
                lanes = slice(one // 2 * 128, one // 2 * 128 + 128)
                q, k = q4[:, lanes], k4[:, lanes]
                if one % 2 == 0:
                    packed = jnp.where(low, q, swap_halves(k))
                else:
                    packed = jnp.where(low, swap_halves(q), k)
                outmsg[head, 0:TOKB] = packed.astype(BF16)
                mine = vt[one * HEAD : (one + 1) * HEAD]
                outmsg[head, TOKB : TOKB + HEAD] = mine[:, :half]
                outmsg[head, TOKB + HEAD : TOKB + 2 * HEAD] = mine[:, half:]

        @pl.when(i == 0)
        def _():
            send_group(0)

        return 0

    lax.fori_loop(0, len(PLANES), project, 0)
    for group in range(1, WINDOW):
        send_group(group)

    def meet(acc, q, k):
        for c in range(2):
            key = keys[k, c * 2 * TOKB : (c + 1) * 2 * TOKB]
            expo = jnp.exp2(dot_nt(key, queries[q]) * LOG2E).astype(BF16)
            acc = acc + dot(values[k * 2 + c], expo)
        return acc

    def stage(i, _):
        @pl.when(i + WINDOW < planes)
        def _():
            sent_group(i)
            send_group(i + WINDOW)

        for one in range(4):
            peer = place(i, one, -1)

            @pl.when(peer != me)
            def _():
                message(peer, peer).wait_recv()

            span = slice(one * TOKB, (one + 1) * TOKB)
            qk = inmsg[peer, 0:TOKB]
            keys[i, span] = qk
            queries[i, span] = jnp.where(low, 0.0, swap_halves(qk.astype(F32))).astype(BF16)
            chunk = i * 2 + one // 2
            base = one % 2 * TOKB
            values[chunk, 0:HEAD, base : base + half] = inmsg[peer, TOKB : TOKB + HEAD]
            values[chunk, 0:HEAD, base + half : base + TOKB] = inmsg[
                peer, TOKB + HEAD : TOKB + 2 * HEAD
            ]

        def pair(t, _):
            q = t

            @pl.when(t < i)
            def _():
                older, newer = accs[t], accs[i]
                older, newer = meet(older, t, i), meet(newer, i, t)
                accs[t] = older
                accs[i] = newer

            @pl.when(t == i)
            def _():
                accs[i] = meet(accs[i], i, i)

            @pl.when(i == planes - 1)
            def _():
                acc = accs[q]
                ctx = (acc[:HEAD] / acc[HEAD : HEAD + 1]).astype(BF16)
                for one in range(4):
                    peer = place(q, one, -1)
                    mine = ctx[:, one * TOKB : (one + 1) * TOKB]

                    @pl.when(peer != me)
                    def _():
                        outctx[peer] = mine
                        remote(
                            outctx.at[peer],
                            inctx.at[me],
                            ctx_send.at[peer],
                            ctx_recv.at[me],
                            "sec",
                            peer,
                        ).start()

                    @pl.when(peer == me)
                    def _():
                        inctx[me] = mine

            return 0

        lax.fori_loop(0, i + 1, pair, 0)
        return 0

    lax.fori_loop(0, planes, stage, 0)

    for group in range(planes - WINDOW, planes):
        sent_group(group)

    def context(peer):
        remote(
            outctx.at[peer], inctx.at[peer], ctx_send.at[peer], ctx_recv.at[peer], "sec", peer
        ).wait()

    each_peer(n, me, context)
    for load in loads[4:]:
        load.wait()

    ctx = jnp.transpose(inctx[...].reshape(D, TOKB))
    mixed = (normed_ref[...].astype(F32) + dot(ctx, out_w[...])).astype(BF16)
    mixed_ref[...] = mixed
    term = cot_t[...].astype(F32) * jax.nn.sigmoid(dot_nt(den_t[...], mixed))
    part = lax.dot_general(
        term,
        mixed.astype(F32),
        (((1,), (0,)), ((), ())),
        precision=lax.Precision.HIGHEST,
        preferred_element_type=F32,
    )
    for p in range(n):
        c, h = p // 2, p % 2
        part_out[p] = part[h * 8 : h * 8 + 8, c * 128 : (c + 1) * 128]

    def send_part(peer):
        remote(
            part_out.at[peer], part_in.at[me], part_send.at[peer], part_recv.at[me], "sec", peer
        ).start()

    each_peer(n, me, send_part)
    part_in[me] = part_out[me]

    density = softplus(dot_nt(mixed, den_t[...]))
    blocks = vox.shape[0]
    for pair in range(HEIGHTS // 2):
        two = dot(mixed_ref[...], vox_w[:, pair * 256 : (pair + 1) * 256])
        vox[:, pair * 16 : pair * 16 + 16, :] = jnp.concatenate(
            [two[:, :128].reshape(blocks, 8, 128), two[:, 128:].reshape(blocks, 8, 128)], axis=1
        ).astype(BF16)
        for one in range(2):
            h = pair * 2 + one
            dens[:, h * 8 : h * 8 + 8, :] = jnp.broadcast_to(
                density[:, h : h + 1], (TOKB, 128)
            ).reshape(blocks, 8, 128)
    bundles = rays.shape[0] // 128
    owned = bundles // n
    factor = 4.0 / (n * KB * 128)

    def render(i, _):
        peers = [lax.rem(me + 2 * i + 1 + one, n) for one in range(2)]
        for peer in peers:
            for y in range(owned):
                bundle = peer * owned + y
                ray = rays[pl.ds(pl.multiple_of(bundle * 128, 128), 128), :]
                picks = [ids[j, bundle] for j in range(KB)]
                score = dot_nt(jnp.concatenate([vox[b] for b in picks], axis=0), ray)
                total = jnp.zeros((8, 128), F32)
                for j in range(KB):
                    value = softplus(score[j * 128 : (j + 1) * 128]) * dens[picks[j]]
                    total = total + jnp.sum(value.reshape(16, 8, 128), axis=0)
                tau_out[peer, y : y + 1, :] = jnp.sum(total, axis=0, keepdims=True) * factor

        for peer in peers:

            @pl.when(peer != me)
            def _():
                remote(
                    tau_out.at[peer], tau_in.at[me], tau_send.at[peer], tau_recv.at[me], "sec", peer
                ).start()

            @pl.when(peer == me)
            def _():
                tau_in[me] = tau_out[me]

        @pl.when(i == 1)
        def _():
            def wait_part(peer):
                remote(
                    part_out.at[peer],
                    part_in.at[peer],
                    part_send.at[peer],
                    part_recv.at[peer],
                    "sec",
                    peer,
                ).wait()

            each_peer(n, me, wait_part)
            row = part_in[0]
            for r in range(1, n):
                row = row + part_in[r]
            row_out[...] = row
            row_in[clip] = row

            def send_row(peer):
                remote(
                    row_out, row_in.at[clip], row_send.at[peer], row_recv.at[clip], "dp", peer
                ).start()

            each_peer(nd, clip, send_row)

        @pl.when(i == 4)
        def _():
            def wait_row(peer):
                remote(
                    row_out, row_in.at[peer], row_send.at[peer], row_recv.at[peer], "dp", peer
                ).wait()

            each_peer(nd, clip, wait_row)
            full = row_in[0]
            for r in range(1, nd):
                full = full + row_in[r]
            full_out[...] = full
            full_in[me] = full

            def send_full(peer):
                remote(
                    full_out, full_in.at[me], full_send.at[peer], full_recv.at[me], "sec", peer
                ).start()

            each_peer(n, me, send_full)

        return 0

    lax.fori_loop(0, n // 2, render, 0)

    def finish(peer):
        remote(
            full_out, full_in.at[peer], full_send.at[peer], full_recv.at[peer], "sec", peer
        ).wait()
        remote(
            tau_out.at[peer], tau_in.at[peer], tau_send.at[peer], tau_recv.at[peer], "sec", peer
        ).wait()

    each_peer(n, me, finish)


def finish_kernel(n, tau_ref, full_ref, depth_ref, grad_ref):
    for p in range(n):
        c, h = p // 2, p % 2
        grad_ref[h * 8 : h * 8 + 8, c * 128 : (c + 1) * 128] = full_ref[p]
    before = jnp.zeros(tau_ref.shape[1:], F32)
    depth = jnp.zeros(tau_ref.shape[1:], F32)
    for r in range(n):
        tau = tau_ref[r]
        depth = depth + (r + 0.5) * jnp.exp(-before) * (1.0 - jnp.exp(-tau))
        before = before + tau
    depth_ref[...] = depth


def any_space():
    return pl.BlockSpec(memory_space=pl.ANY)


def vmem():
    return pl.BlockSpec(memory_space=pltpu.VMEM)


def dma(count):
    return pltpu.SemaphoreType.DMA((count,))


def shards(
    range_features,
    conv_weight,
    cell_cycle,
    cell_token,
    in_weight,
    qkv_weight,
    out_weight,
    voxel_weight,
    density_weight,
    ray_embed,
    block_ids,
    density_cotangent,
):
    _, az_dev, beams, width = range_features.shape
    n, nd = lax.axis_size("sec"), lax.axis_size("dp")
    cells = az_dev * beams
    bundles = ray_embed.shape[0] // 128
    owned = bundles // n
    blocks = TOKB * HEIGHTS // 128
    message = (n, TOKB + TOKB // 2, 128)
    tau, full = pl.pallas_call(
        functools.partial(forecast_kernel, n, nd, cells, beams),
        out_shape=(
            jax.ShapeDtypeStruct((n, owned, 128), F32),
            jax.ShapeDtypeStruct((n, 8, 128), F32),
        ),
        in_specs=[pl.BlockSpec(memory_space=pltpu.SMEM)] + [vmem()] * 4 + [any_space()] * 7,
        out_specs=(vmem(), vmem()),
        scratch_shapes=[
            pltpu.VMEM((1, cells), jnp.int32),
            pltpu.VMEM((cells + 2 * beams, width), BF16),
            pltpu.VMEM((cells, width), BF16),
            pltpu.VMEM((4, 4, TOKB, width // 2), BF16),
            pltpu.VMEM((4, 4, TOKB, width // 2), BF16),
            pltpu.VMEM((4, 4, TOKB, width // 2), BF16),
            pltpu.VMEM((4, 4, TOKB, width // 2), BF16),
            pltpu.VMEM((2, 4, TOKB, width // 2), F32),
            pltpu.VMEM((2, 4, TOKB, width // 2), F32),
            pltpu.VMEM((n, 1, TOKB), F32),
            pltpu.VMEM((n, 1, TOKB), F32),
            pltpu.VMEM(message, BF16),
            pltpu.VMEM(message, BF16),
            pltpu.VMEM((TOKB, D), BF16),
            pltpu.VMEM((n // 4, 4 * TOKB, 128), BF16),
            pltpu.VMEM((n // 4, 4 * TOKB, 128), BF16),
            pltpu.VMEM((n // 2, HEAD + 16, 2 * TOKB), BF16),
            pltpu.VMEM((n // 4, HEAD + 16, 4 * TOKB), F32),
            pltpu.VMEM((n, HEAD, TOKB), BF16),
            pltpu.VMEM((n, HEAD, TOKB), BF16),
            pltpu.VMEM((TOKB, D), BF16),
            pltpu.VMEM((blocks, 128, EMB), BF16),
            pltpu.VMEM((blocks, 128, 128), F32),
            pltpu.VMEM((n, owned, 128), F32),
            pltpu.VMEM((n, 8, 128), F32),
            pltpu.VMEM((n, 8, 128), F32),
            pltpu.VMEM((8, 128), F32),
            pltpu.VMEM((nd, 8, 128), F32),
            pltpu.VMEM((8, 128), F32),
            pltpu.VMEM(conv_weight.shape, BF16),
            pltpu.VMEM(in_weight.shape, BF16),
            pltpu.VMEM(qkv_weight.shape, BF16),
            pltpu.VMEM(out_weight.shape, BF16),
            pltpu.VMEM(voxel_weight.shape, BF16),
            pltpu.VMEM(ray_embed.shape, BF16),
            dma(7),
            dma(2),
            dma(2),
            dma(32),
            dma(32),
            dma(8),
            dma(8),
            dma(n),
            dma(n),
            dma(n),
            dma(n),
            dma(n),
            dma(n),
            dma(n),
            dma(n),
            dma(n),
            dma(n),
            dma(nd),
            dma(nd),
            dma(n),
            dma(n),
        ],
        compiler_params=pltpu.CompilerParams(
            collective_id=0, has_side_effects=True, vmem_limit_bytes=VMEM_LIMIT
        ),
        name="forecast",
    )(
        block_ids[0].T,
        cell_cycle.reshape(az_dev, beams),
        cell_token,
        density_weight.T,
        density_cotangent[0].T,
        range_features.reshape(cells, width),
        conv_weight,
        in_weight,
        qkv_weight,
        out_weight,
        voxel_weight,
        ray_embed,
    )
    depth, grad = pl.pallas_call(
        functools.partial(finish_kernel, n),
        out_shape=(
            jax.ShapeDtypeStruct((owned, 128), F32),
            jax.ShapeDtypeStruct((HEIGHTS, D), F32),
        ),
        in_specs=[vmem(), vmem()],
        out_specs=(vmem(), vmem()),
        name="finish",
    )(tau, full)
    return depth.reshape(1, owned * 128), grad


def solution(mesh):
    placed = (
        P("dp", "sec", None, None),
        P(),
        P("sec", None, None),
        P("sec", None),
        P(),
        P(),
        P(),
        P(),
        P(),
        P(),
        P("sec", None, None),
        P("dp", "sec", None),
    )
    return jax.shard_map(
        shards, mesh=mesh, in_specs=placed, out_specs=(P("dp", "sec"), P()), check_vma=False
    )
```
